256 devices in a mesh: dp: 64 (over z_hi, x, y, core), mp: 4 (over z_lo).
Axes of the slice: x: 4, y: 4, z: 8 (z_hi: 2, z_lo: 4; z = z_hi * 4 + z_lo), core: 2. Of those that a mesh axis runs over, the one named last changes fastest.
Arguments:
- activations: bfloat16 [49152, 4096], P('dp', 'mp'), may hold values from -16 to 16
- out_grads: bfloat16 [49152, 4096], P('dp', 'mp'), may hold values from -0.125 to 0.125
- weight: float32 [4096, 4096], P('dp', 'mp'), may hold values from -0.09375 to 0.09375
- row_moment: float32 [4096], P('dp'), may hold values from 0.05 to 2
- col_moment: float32 [4096], P('mp'), may hold values from 0.05 to 2
Outputs:
- new_weight: float32 [4096, 4096], P('dp', 'mp')
- update: float32 [4096, 4096], P('dp', 'mp')
- new_row: float32 [4096], P('dp')
- new_col: float32 [4096], P('mp')
The draws below stay inside these ranges and needn't reach their ends.
All inputs are finite; a program needn't handle non-finite values.
Results may differ from the reference program's by a relative error of at most 0.0003.
Values may be sent and summed in bfloat16 or wider, within the bound.
A program may use at most 64 MiB of HBM per device.

```python
import math
import jax
import jax.numpy as jnp
from jax import lax

D = 4096
STEPS_DONE = 10
TOKENS = 49152


def with_spikes(entries, own_key, source, target, shards_of, factor):
    def block_of(dim):
        return (jnp.arange(entries.shape[dim]) // (entries.shape[dim] // shards_of)).reshape((-1,) + (1,) * (entries.ndim - 1 - dim))

    one_side = jax.random.permutation(own_key, shards_of)[block_of(target)]
    other_side = (block_of(target) + shards_of // 2) % shards_of
    return jnp.where((block_of(source) == one_side) | (block_of(source) == other_side), factor * entries, entries)


def levels(own_key, shape, cuts, low, top_value):
    def one(axis_at, shards_of):
        draws = jax.random.uniform(jax.random.fold_in(jax.random.fold_in(own_key, 6), axis_at), (shards_of,), jnp.float32, low / len(cuts), top_value / len(cuts))
        return jnp.repeat(jnp.exp(draws), shape[axis_at] // shards_of).reshape((-1,) + (1,) * (len(shape) - axis_at - 1))

    loudness = one(*cuts[0])
    for cut in cuts[1:]:
        loudness = loudness * one(*cut)
    return loudness


def normal_values(rng, dims, width, bound, split=(), dtype=jnp.bfloat16):
    drawn = jax.random.normal(rng, dims, jnp.float32) * width
    if len(split) > 0:
        drawn = levels(rng, dims, split, -0.22, 0.18) * drawn
    return jnp.clip(drawn, min=-bound, max=bound).astype(dtype)


def noise_with(own_key, dims, scale, bound, split, heavy, dtype=jnp.bfloat16):
    values = scale * jax.random.normal(own_key, dims, jnp.float32)
    if split:
        values = values * levels(own_key, dims, split, -0.22, 0.18)
    return jnp.clip(with_spikes(values, jax.random.fold_in(own_key, 3), *heavy), -bound, bound).astype(dtype)


def setup_inputs(seed: int = 0) -> dict:
    key_of = jax.random.split(jax.random.key(seed), 6)
    activations = noise_with(key_of[0], (TOKENS, D), 1.0, 16.0, ((0, 64), (1, 4)), (0, 1, 64, 4.0))
    out_grads = normal_values(key_of[1], (TOKENS, D), (2.0 * TOKENS ** -0.5), 0.125, ((0, 64), (1, 4)))
    weight = normal_values(key_of[2], (D, D), D ** -0.5, 0.09375, ((0, 64), (1, 4)), jnp.float32)
    row_moment = jnp.clip(jnp.exp(math.log(2.0) - 3.6888794 * jax.random.uniform(key_of[3], (D,), jnp.float32) ** levels(key_of[3], (D,), ((0, 64),), -0.2, 0.2)), 0.05, 2.0)
    col_moment = jnp.clip(jnp.exp(math.log(2.0) - 3.6888794 * jax.random.uniform(key_of[4], (D,), jnp.float32) ** levels(key_of[4], (D,), ((0, 4),), -0.2, 0.2)), 0.05, 2.0)
    return {"activations": activations, "out_grads": out_grads, "weight": weight, "row_moment": row_moment, "col_moment": col_moment}


learn_rate = 0.01
tiny_eps = 1e-30

def reference(activations, out_grads, weight, row_moment, col_moment):
    gradient = lax.dot_general(activations, out_grads, (((0,), (0,)), ((), ())), preferred_element_type=jnp.float32)
    decay = 1.0 - STEPS_DONE ** (-0.8)
    squared = gradient * gradient + tiny_eps
    new_row = decay * row_moment + (1.0 - decay) * lax.optimization_barrier(jnp.mean(squared, axis=1))
    new_col = decay * col_moment + (1.0 - decay) * lax.optimization_barrier(jnp.mean(squared, axis=0))
    scale_total = jnp.mean(new_row)
    scaled = gradient / jnp.sqrt(new_row[:, None] * new_col[None, :] / scale_total)
    root_mean = jnp.sqrt(jnp.mean(scaled * scaled))
    update = scaled / jnp.maximum(1.0, root_mean)
    new_weight = weight - learn_rate * update
    return (new_weight, update, new_row, new_col)
```

```python
import jax
import jax.numpy as jnp
from jax import lax
from jax.experimental import pallas as pl
from jax.experimental.pallas import tpu as pltpu
from jax.sharding import PartitionSpec as P

D = 4096
STEPS_DONE = 10
MESH = pl.DeviceIdType.MESH

learn_rate = 0.01
tiny_eps = 1e-30
DECAY = 1.0 - STEPS_DONE ** (-0.8)

TOK = 768
FEAT = 1024
STEPS = 8
WIDE = 256
ROWS = 64


def kernel(
    a_ref, b_ref, w_ref, rm_ref, cm_ref,
    nw_ref, up_ref, nr_ref, nc_ref,
    aa, bb, ps, own, give, take, in1, mid, in2, res, fin, grad,
    row_in, col_mine, col_in, col_mid, col_in2, sca_mine, sca_in, sca_mid, sca_in2,
    s_a, r_a, s_b1, r_b1, s_b2, r_b2, r_ps, s_fw,
    s_core, r_core, s_1, r_1, s_2, r_2, s_z, r_z,
    s_row, r_row, s_col, r_col, s_col2, r_col2, s_sca, r_sca, s_sca2, r_sca2,
):
    d = lax.axis_index("dp")
    c = lax.axis_index("mp")
    zh, x, y, core = d // 32, (d // 8) % 4, (d // 2) % 4, d % 2

    def dev(zh_, x_, y_, core_, c_):
        return (((zh_ * 4 + x_) * 4 + y_) * 2 + core_, c_)

    def plane_peer(j):
        q = lax.rem(x * 4 + y + j, 16)
        return dev(zh, q // 4, q % 4, core, c)

    def pole_peer(j):
        q = lax.rem((zh * 4 + c) * 2 + core + j, 16)
        return dev(q // 8, x, y, q % 2, (q // 2) % 4)

    def send(src, dst, s_sem, r_sem, to):
        return pltpu.make_async_remote_copy(
            src_ref=src, dst_ref=dst, send_sem=s_sem, recv_sem=r_sem, device_id=to, device_id_type=MESH
        )

    barrier = pltpu.get_barrier_semaphore()

    def greet(j, _):
        pl.semaphore_signal(barrier, inc=1, device_id=plane_peer(j), device_id_type=MESH)
        pl.semaphore_signal(barrier, inc=1, device_id=pole_peer(j), device_id_type=MESH)
        return 0

    lax.fori_loop(1, 16, greet, 0)
    pl.semaphore_wait(barrier, 30)

    edge = (c == 0) | (c == 3)
    half = lax.rem(c, 2)
    to_pair = dev(zh, x, y, core, c + 1 - 2 * half)
    to_mid = dev(zh, x, y, core, 3 - c)

    def a_copy(i):
        return send(a_ref.at[:, pl.ds(512 * i, 512)], aa.at[2 * half + i], s_a.at[i], r_a.at[i], to_pair)

    def b1_copy(i):
        return send(b_ref.at[:, pl.ds(WIDE * i, WIDE)], bb.at[i], s_b1.at[i], r_b1.at[i], to_mid)

    def b_piece(i):
        return b_ref.at[:, pl.ds(128 * i, 128)]

    def bb_piece(i):
        return bb.at[4 + i // 2, :, pl.ds(128 * (i % 2), 128)]

    def ps_piece(i):
        return ps.at[i // 2, :, pl.ds(128 * (i % 2), 128)]

    def b2_copy(i):
        return send(b_piece(i), bb_piece(i), s_b2.at[i], r_b2.at[i], to_pair)

    def ps_copy(i):
        return send(b_piece(i), ps_piece(i), s_b2.at[i], r_ps.at[i], to_pair)

    def fw_copy(i):
        return send(ps_piece(i), bb_piece(i), s_fw.at[i], r_b2.at[i], to_mid)

    @pl.when(edge)
    def _():
        for i in range(2):
            a_copy(i).start()
        for i in range(8):
            ps_copy(i).start()

    @pl.when(jnp.logical_not(edge))
    def _():
        for i in range(2):
            a_copy(i).start()
            b1_copy(2 * i).start()
            b1_copy(2 * i + 1).start()
        for i in range(8):
            b2_copy(i).start()

    for i in range(2):
        aa[2 * half + i] = a_ref[:, pl.ds(512 * i, 512)]

    @pl.when(edge)
    def _():
        for i in range(4):
            bb[i] = b_ref[:, pl.ds(WIDE * i, WIDE)]

    for i in range(2):
        send(a_ref.at[:, pl.ds(512 * i, 512)], aa.at[2 * (1 - half) + i], s_a.at[i], r_a.at[i], to_pair).wait_recv()

    def forward(i):
        @pl.when(jnp.logical_not(edge))
        def _():
            for k in range(8):
                @pl.when(i == k)
                def _():
                    ps_copy(k).wait_recv()
                    fw_copy(k).start()

    def core_copy(t):
        return send(give.at[t % 2], take.at[t], s_core.at[t], r_core.at[t], dev(zh, x, y, 1 - core, c))

    def multiply(t):
        @pl.when((t < 4) & jnp.logical_not(edge))
        def _():
            for k in range(4):
                @pl.when(t == k)
                def _():
                    b1_copy(k).wait_recv()

        for k in range(4, 8):
            @pl.when(t == k)
            def _():
                b2_copy(2 * (k - 4)).wait_recv()
                b2_copy(2 * (k - 4) + 1).wait_recv()

        @pl.when(t >= 2)
        def _():
            core_copy(t - 2).wait_send()

        def of_x(xx, _):
            r = lax.dot_general(
                aa[xx], bb[t], (((0,), (0,)), ((), ())), preferred_element_type=jnp.float32
            )
            for yy in range(4):
                lo, hi = r[128 * yy : 128 * yy + 64], r[128 * yy + 64 : 128 * yy + 128]
                keep, go = jnp.where(core == 0, lo, hi), jnp.where(core == 0, hi, lo)
                own[t, 0, xx, yy] = keep[:, :128]
                own[t, 1, yy, xx] = keep[:, 128:]
                give[t % 2, 0, xx, yy] = go[:, :128]
                give[t % 2, 1, yy, xx] = go[:, 128:]
            return 0

        lax.fori_loop(0, 4, of_x, 0)
        core_copy(t).start()

    def copies_1(t):
        out = []
        for j in range(1, 4):
            out.append(send(own.at[t, 0, lax.rem(x + j, 4)], in1.at[t, 0, j - 1], s_1.at[t, 0, j - 1],
                            r_1.at[t, 0, j - 1], dev(zh, lax.rem(x + j, 4), y, core, c)))
            out.append(send(own.at[t, 1, lax.rem(y + j, 4)], in1.at[t, 1, j - 1], s_1.at[t, 1, j - 1],
                            r_1.at[t, 1, j - 1], dev(zh, x, lax.rem(y + j, 4), core, c)))
        return out

    def add_cores(t):
        core_copy(t).wait_recv()

        def of(k, _):
            own[t, k // 4, k % 4] += take[t, k // 4, k % 4]
            return 0

        lax.fori_loop(0, 8, of, 0)
        for q in copies_1(t):
            q.start()

    def copies_2(t):
        out = []
        for j in range(1, 4):
            out.append(send(mid.at[t, 0, lax.rem(y + j, 4)], in2.at[t, 0, j - 1], s_2.at[t, 0, j - 1],
                            r_2.at[t, 0, j - 1], dev(zh, x, lax.rem(y + j, 4), core, c)))
            out.append(send(mid.at[t, 1, lax.rem(x + j, 4)], in2.at[t, 1, j - 1], s_2.at[t, 1, j - 1],
                            r_2.at[t, 1, j - 1], dev(zh, lax.rem(x + j, 4), y, core, c)))
        return out

    def add_first(t):
        for q in copies_1(t):
            q.wait_recv()
        mid[t, 0] = own[t, 0, x] + in1[t, 0, 0] + in1[t, 0, 1] + in1[t, 0, 2]
        mid[t, 1] = own[t, 1, y] + in1[t, 1, 0] + in1[t, 1, 1] + in1[t, 1, 2]
        for q in copies_2(t):
            q.start()

    def target(t):
        return jnp.where(t < 4, jnp.where(edge, c, 3 - c), lax.rem(2 * c + 1, 5))

    def stays(t):
        return (zh == c // 2) & (target(t) == c)

    def z_copy(t):
        return send(res.at[t], fin.at[zh, lax.rem(t, 4)], s_z.at[t], r_z.at[zh, lax.rem(t, 4)],
                    dev(c // 2, x, y, core, target(t)))

    def add_second(t):
        for q in copies_2(t):
            q.wait_recv()
        lo = mid[t, 0, y] + in2[t, 0, 0] + in2[t, 0, 1] + in2[t, 0, 2]
        hi = mid[t, 1, x] + in2[t, 1, 0] + in2[t, 1, 1] + in2[t, 1, 2]

        @pl.when(stays(t))
        def _():
            fin[zh, lax.rem(t, 4), :, :128] = lo
            fin[zh, lax.rem(t, 4), :, 128:] = hi

        @pl.when(jnp.logical_not(stays(t)))
        def _():
            res[t, :, :128] = lo
            res[t, :, 128:] = hi
            z_copy(t).start()

    def step(s, _):
        @pl.when(s < 8)
        def _():
            @pl.when(s >= 6)
            def _():
                forward(s)

            multiply(s)

            @pl.when(s < 6)
            def _():
                forward(s)

        @pl.when((s >= 1) & (s < 9))
        def _():
            add_cores(s - 1)

        @pl.when((s >= 2) & (s < 10))
        def _():
            add_first(s - 2)

        @pl.when(s >= 3)
        def _():
            add_second(s - 3)

        return 0

    lax.fori_loop(0, 11, step, 0)

    source = 2 * zh + c // 2
    for g in range(2):
        for k in range(4):
            @pl.when(jnp.logical_not((zh == g) & (source == c)))
            def _():
                send(res.at[k], fin.at[g, k], s_z.at[k], r_z.at[g, k], dev(g, x, y, core, source)).wait_recv()
    col_sum = []
    row_sum = jnp.zeros((ROWS, 128), jnp.float32)
    for k in range(4):
        g = fin[0, k] + fin[1, k]
        grad[:, pl.ds(WIDE * k, WIDE)] = g
        sq = g * g + tiny_eps
        row_sum = row_sum + sq[:, :128] + sq[:, 128:]
        col_mine[:, pl.ds(WIDE * k, WIDE)] = jnp.sum(sq, axis=0, keepdims=True)
    row_in[0] = row_sum

    def row_copy(j):
        return send(row_in.at[0], row_in.at[j], s_row.at[j - 1], r_row.at[j - 1], dev(zh, x, y, core, lax.rem(c + j, 4)))

    def col_copy(j):
        return send(col_mine, col_in.at[j - 1], s_col.at[j - 1], r_col.at[j - 1], plane_peer(j))

    def col_copy2(j):
        q = lax.rem(zh * 2 + core + j, 4)
        return send(col_mid, col_in2.at[j - 1], s_col2.at[j - 1], r_col2.at[j - 1], dev(q // 2, x, y, q % 2, c))

    def each(lo, hi, f):
        def one(j, _):
            f(j)
            return 0
        lax.fori_loop(lo, hi, one, 0)

    each(1, 16, lambda j: col_copy(j).start())
    each(1, 4, lambda j: row_copy(j).start())
    each(1, 16, lambda j: col_copy(j).wait_recv())
    total = col_mine[...]
    for j in range(15):
        total = total + col_in[j]
    col_mid[...] = total
    each(1, 4, lambda j: col_copy2(j).start())
    each(1, 4, lambda j: row_copy(j).wait_recv())
    rows = jnp.sum(row_in[0] + row_in[1] + row_in[2] + row_in[3], axis=1, keepdims=True)
    eye = lax.broadcasted_iota(jnp.int32, (ROWS, ROWS), 0) == lax.broadcasted_iota(jnp.int32, (ROWS, ROWS), 1)
    rm = jnp.sum(jnp.where(eye, rm_ref[...], 0.0), axis=1, keepdims=True)
    new_row = DECAY * rm + (1.0 - DECAY) * (rows / D)
    nr_ref[...] = jnp.sum(jnp.where(eye, new_row, 0.0), axis=0, keepdims=True)
    each(1, 4, lambda j: col_copy2(j).wait_recv())
    cols = col_mid[...] + col_in2[0] + col_in2[1] + col_in2[2]
    new_col = DECAY * cm_ref[...] + (1.0 - DECAY) * (cols / D)
    nc_ref[...] = new_col
    root_r = 1.0 / jnp.sqrt(new_row)
    root_c = 1.0 / jnp.sqrt(new_col)
    scaled = grad[...] * root_r * root_c
    part = jnp.sum(scaled * scaled)
    row_part = jnp.sum(new_row)
    lane = lax.broadcasted_iota(jnp.int32, (8, 128), 1)
    sca_mine[...] = jnp.where(lane == 0, part, jnp.where(lane == 1, row_part, 0.0))

    def sca_copy(j):
        return send(sca_mine, sca_in.at[j - 1], s_sca.at[j - 1], r_sca.at[j - 1], plane_peer(j))

    def sca_copy2(j):
        return send(sca_mid, sca_in2.at[j - 1], s_sca2.at[j - 1], r_sca2.at[j - 1], pole_peer(j))

    each(1, 16, lambda j: sca_copy(j).start())
    each(1, 16, lambda j: sca_copy(j).wait_recv())
    total = sca_mine[...]
    for j in range(15):
        total = total + sca_in[j]
    sca_mid[...] = total
    each(1, 16, lambda j: sca_copy2(j).start())
    each(1, 16, lambda j: sca_copy2(j).wait_recv())
    total = sca_mid[...]
    for j in range(15):
        total = total + sca_in2[j]
    sum_sq = jnp.sum(jnp.where(lane == 0, total, 0.0), axis=1, keepdims=True)[:1]
    sum_row = jnp.sum(jnp.where(lane == 1, total, 0.0), axis=1, keepdims=True)[:1] / 4.0
    scale_total = sum_row / D
    root_mean = jnp.sqrt(sum_sq * scale_total / (D * D))
    factor = jnp.sqrt(scale_total) / jnp.maximum(1.0, root_mean)
    update = grad[...] * (root_r * factor) * root_c
    up_ref[...] = update
    nw_ref[...] = w_ref[...] - learn_rate * update

    for i in range(2):
        a_copy(i).wait_send()
    for i in range(8):
        b2_copy(i).wait_send()

    @pl.when(jnp.logical_not(edge))
    def _():
        for i in range(4):
            b1_copy(i).wait_send()
        for i in range(8):
            fw_copy(i).wait_send()

    core_copy(6).wait_send()
    core_copy(7).wait_send()

    def sent(t):
        for q in copies_1(t) + copies_2(t):
            q.wait_send()

        @pl.when(jnp.logical_not(stays(t)))
        def _():
            z_copy(t).wait_send()

    each(0, 8, sent)
    each(1, 4, lambda j: row_copy(j).wait_send())
    each(1, 16, lambda j: col_copy(j).wait_send())
    each(1, 4, lambda j: col_copy2(j).wait_send())
    each(1, 16, lambda j: sca_copy(j).wait_send())
    each(1, 16, lambda j: sca_copy2(j).wait_send())


def body(activations, out_grads, weight, row_moment, col_moment):
    f32, bf16 = jnp.float32, jnp.bfloat16
    V, S = pltpu.VMEM, pltpu.SemaphoreType.DMA
    vmem = pl.BlockSpec(memory_space=pltpu.VMEM)
    buffers = [
        V((4, TOK, 512), bf16),
        V((8, TOK, WIDE), bf16),
        V((4, TOK, WIDE), bf16),
        V((STEPS, 2, 4, 4, ROWS, 128), f32),
        V((2, 2, 4, 4, ROWS, 128), f32),
        V((STEPS, 2, 4, 4, ROWS, 128), f32),
        V((STEPS, 2, 3, 4, ROWS, 128), f32),
        V((STEPS, 2, 4, ROWS, 128), f32),
        V((STEPS, 2, 3, ROWS, 128), f32),
        V((STEPS, ROWS, WIDE), f32),
        V((2, 4, ROWS, WIDE), f32),
        V((ROWS, FEAT), f32),
        V((4, ROWS, 128), f32),
        V((1, FEAT), f32), V((15, 1, FEAT), f32), V((1, FEAT), f32), V((3, 1, FEAT), f32),
        V((8, 128), f32), V((15, 8, 128), f32), V((8, 128), f32), V((15, 8, 128), f32),
    ]
    sems = [S((2,)), S((2,)), S((4,)), S((4,)), S((8,)), S((8,)), S((8,)), S((8,)),
            S((8,)), S((8,)), S((8, 2, 3)), S((8, 2, 3)), S((8, 2, 3)), S((8, 2, 3)), S((8,)), S((2, 4)),
            S((3,)), S((3,)), S((15,)), S((15,)), S((3,)), S((3,)), S((15,)), S((15,)), S((15,)), S((15,))]
    nw, up, nr, nc = pl.pallas_call(
        kernel,
        out_shape=[
            jax.ShapeDtypeStruct((ROWS, FEAT), f32),
            jax.ShapeDtypeStruct((ROWS, FEAT), f32),
            jax.ShapeDtypeStruct((1, ROWS), f32),
            jax.ShapeDtypeStruct((1, FEAT), f32),
        ],
        in_specs=[vmem] * 5,
        out_specs=[vmem] * 4,
        scratch_shapes=buffers + sems,
        compiler_params=pltpu.CompilerParams(
            collective_id=0, has_side_effects=True, vmem_limit_bytes=60 * 2**20
        ),
    )(activations, out_grads, weight, row_moment.reshape(1, ROWS), col_moment.reshape(1, FEAT))
    return nw, up, nr.reshape(ROWS), nc.reshape(FEAT)


def solution(mesh):
    return jax.shard_map(
        body,
        mesh=mesh,
        in_specs=(P("dp", "mp"), P("dp", "mp"), P("dp", "mp"), P("dp"), P("mp")),
        out_specs=(P("dp", "mp"), P("dp", "mp"), P("dp"), P("mp")),
        check_vma=False,
    )
```

```python
import jax
import jax.numpy as jnp
from jax import lax
from jax.experimental import pallas as pl
from jax.experimental.pallas import tpu as pltpu
from jax.sharding import PartitionSpec as P

D = 4096
STEPS_DONE = 10
MESH = pl.DeviceIdType.MESH

learn_rate = 0.01
tiny_eps = 1e-30
DECAY = 1.0 - STEPS_DONE ** (-0.8)

TOK = 768
FEAT = 1024
STEPS = 8
WIDE = 256
ROWS = 64


POWER = 16
TOP = 239.0


def coded(v):
    most = jnp.max(jnp.abs(v), axis=0, keepdims=True)
    scale = (most * 1.01 + 1e-30).astype(jnp.bfloat16)
    u = v * (TOP / scale.astype(jnp.float32))
    m = u * u
    m = m * m
    m = m * m
    m = m * m
    y = jnp.where(u < 0.0, -m, m).astype(jnp.bfloat16)
    return y, jnp.broadcast_to(scale, (16, v.shape[1]))


def decoded(y, scale):
    f = y.astype(jnp.float32)
    m = jnp.exp(jnp.log(jnp.abs(f)) * (1.0 / POWER))
    return jnp.where(f < 0.0, -m, m) * (scale.astype(jnp.float32)[:1] * (1.0 / TOP))


def kernel(
    a_ref, b_ref, rm_ref, cm_ref,
    grad_out, by_row_ref, by_col_ref, nr_ref, nc_ref,
    aa, bb, ps, own, give, take, enc, in1, mid, in2, res, fin, grad,
    row_in, col_mine, col_in, col_mid, col_in2, sca_mine, sca_in, sca_mid, sca_in2,
    s_loc, s_a, r_a, s_b1, r_b1, s_b2, r_b2, r_ps, s_fw,
    s_core, r_core, s_1, r_1, s_2, r_2, s_z, r_z, s_row, s_col, r_row, r_col, s_col2, r_col2, s_sca, r_sca, s_sca2, r_sca2,
):
    d = lax.axis_index("dp")
    c = lax.axis_index("mp")
    zh, x, y, core = d // 32, (d // 8) % 4, (d // 2) % 4, d % 2

    def dev(zh_, x_, y_, core_, c_):
        return (((zh_ * 4 + x_) * 4 + y_) * 2 + core_, c_)

    def plane_peer(j):
        q = lax.rem(x * 4 + y + j, 16)
        return dev(zh, q // 4, q % 4, core, c)

    def pole_peer(j):
        q = lax.rem((zh * 4 + c) * 2 + core + j, 16)
        return dev(q // 8, x, y, q % 2, (q // 2) % 4)

    def send(src, dst, s_sem, r_sem, to):
        return pltpu.make_async_remote_copy(
            src_ref=src, dst_ref=dst, send_sem=s_sem, recv_sem=r_sem, device_id=to, device_id_type=MESH
        )

    def arrived(ref, sem):
        pltpu.make_async_copy(ref, ref, sem).wait()

    barrier = pltpu.get_barrier_semaphore()

    def greet(j, _):
        pl.semaphore_signal(barrier, inc=1, device_id=plane_peer(j), device_id_type=MESH)
        pl.semaphore_signal(barrier, inc=1, device_id=pole_peer(j), device_id_type=MESH)
        return 0

    lax.fori_loop(1, 16, greet, 0)
    pl.semaphore_wait(barrier, 30)

    edge = (c == 0) | (c == 3)
    half = lax.rem(c, 2)
    to_pair = dev(zh, x, y, core, c + 1 - 2 * half)
    to_mid = dev(zh, x, y, core, 3 - c)

    def a_copy(i):
        return send(a_ref.at[:, pl.ds(512 * i, 512)], aa.at[2 * half + i], s_a, r_a, to_pair)

    def b1_copy(i):
        return send(b_ref.at[:, pl.ds(WIDE * i, WIDE)], bb.at[i], s_b1, r_b1.at[i], to_mid)

    def b_piece(i):
        return b_ref.at[:, pl.ds(128 * i, 128)]

    def bb_piece(i):
        return bb.at[4 + i // 2, :, pl.ds(128 * (i % 2), 128)]

    def ps_piece(i):
        return ps.at[i // 2, :, pl.ds(128 * (i % 2), 128)]

    def b2_copy(i):
        return send(b_piece(i), bb_piece(i), s_b2, r_b2.at[i // 2], to_pair)

    def ps_copy(i):
        return send(b_piece(i), ps_piece(i), s_b2, r_ps.at[i], to_pair)

    def fw_copy(i):
        return send(ps_piece(i), bb_piece(i), s_fw, r_b2.at[i // 2], to_mid)

    @pl.when(edge)
    def _():
        for i in range(2):
            a_copy(i).start()
        for i in range(8):
            ps_copy(i).start()

    @pl.when(jnp.logical_not(edge))
    def _():
        for i in range(2):
            a_copy(i).start()
            b1_copy(2 * i).start()
            b1_copy(2 * i + 1).start()
        for i in range(8):
            b2_copy(i).start()

    def a_local(i):
        return pltpu.make_async_copy(a_ref.at[:, pl.ds(512 * i, 512)], aa.at[2 * half + i], s_loc.at[i])

    def b_local(i):
        return pltpu.make_async_copy(b_ref.at[:, pl.ds(WIDE * i, WIDE)], bb.at[i], s_loc.at[2 + i])

    for i in range(2):
        a_local(i).start()

    @pl.when(edge)
    def _():
        for i in range(4):
            b_local(i).start()
        for i in range(4):
            b_local(i).wait()

    for i in range(2):
        a_local(i).wait()
    arrived(aa.at[pl.ds(0, 2)], r_a)

    def forward(i):
        @pl.when(jnp.logical_not(edge))
        def _():
            for k in range(8):
                @pl.when(i == k)
                def _():
                    ps_copy(k).wait_recv()
                    fw_copy(k).start()

    def core_copy(t):
        return send(give.at[t % 2], take.at[t], s_core.at[t % 2], r_core.at[t], dev(zh, x, y, 1 - core, c))

    def multiply(t):
        @pl.when((t < 4) & jnp.logical_not(edge))
        def _():
            for k in range(4):
                @pl.when(t == k)
                def _():
                    b1_copy(k).wait_recv()

        for k in range(4, 8):
            @pl.when(t == k)
            def _():
                arrived(bb.at[k], r_b2.at[k - 4])

        @pl.when(t >= 2)
        def _():
            core_copy(t - 2).wait_send()

        def of_x(xx, _):
            r = lax.dot_general(
                aa[xx], bb[t], (((0,), (0,)), ((), ())), preferred_element_type=jnp.float32
            )
            for yy in range(4):
                lo, hi = r[128 * yy : 128 * yy + 64], r[128 * yy + 64 : 128 * yy + 128]
                keep, go = jnp.where(core == 0, lo, hi), jnp.where(core == 0, hi, lo)
                own[t, 0, xx, yy] = keep[:, :128]
                own[t, 1, yy, xx] = keep[:, 128:]
                give[t % 2, 0, xx, yy] = go[:, :128]
                give[t % 2, 1, yy, xx] = go[:, 128:]
            return 0

        lax.fori_loop(0, 4, of_x, 0)
        core_copy(t).start()

    def copies_1(t):
        out = []
        for j in range(1, 4):
            out.append(send(enc.at[t, 0, lax.rem(x + j, 4)], in1.at[t, 0, j - 1], s_1.at[t], r_1.at[t],
                            dev(zh, lax.rem(x + j, 4), y, core, c)))
            out.append(send(enc.at[t, 1, lax.rem(y + j, 4)], in1.at[t, 1, j - 1], s_1.at[t], r_1.at[t],
                            dev(zh, x, lax.rem(y + j, 4), core, c)))
        return out

    def add_cores(t):
        core_copy(t).wait_recv()

        def of(k, _):
            v = own[t, k // 4, k % 4] + take[t, k // 4, k % 4]
            own[t, k // 4, k % 4] = v
            code, scale = coded(v.reshape(4 * ROWS, 128))
            enc[t, k // 4, k % 4, : 4 * ROWS] = code
            enc[t, k // 4, k % 4, 4 * ROWS :] = scale
            return 0

        lax.fori_loop(0, 8, of, 0)
        for q in copies_1(t):
            q.start()

    def copies_2(t):
        out = []
        for j in range(1, 4):
            out.append(send(mid.at[t, 0, lax.rem(y + j, 4)], in2.at[t, 0, j - 1], s_2.at[t], r_2.at[t], dev(zh, x, lax.rem(y + j, 4), core, c)))
            out.append(send(mid.at[t, 1, lax.rem(x + j, 4)], in2.at[t, 1, j - 1], s_2.at[t], r_2.at[t], dev(zh, lax.rem(x + j, 4), y, core, c)))
        return out

    def add_first(t):
        arrived(in1.at[t], r_1.at[t])

        def of(h, _):
            total = own[t, h, jnp.where(h == 0, x, y)].reshape(4 * ROWS, 128)
            for k in range(3):
                total = total + decoded(in1[t, h, k, : 4 * ROWS], in1[t, h, k, 4 * ROWS :])
            mid[t, h] = total.reshape(4, ROWS, 128)
            return 0

        lax.fori_loop(0, 2, of, 0)
        for q in copies_2(t):
            q.start()

    def target(t):
        return jnp.where(t < 4, jnp.where(edge, c, 3 - c), lax.rem(2 * c + 1, 5))

    def stays(t):
        return (zh == c // 2) & (target(t) == c)

    def z_copy(t):
        return send(res.at[t], fin.at[zh, lax.rem(t, 4)], s_z, r_z.at[zh],
                    dev(c // 2, x, y, core, target(t)))

    def add_second(t):
        arrived(in2.at[t], r_2.at[t])
        lo = mid[t, 0, y] + in2[t, 0, 0] + in2[t, 0, 1] + in2[t, 0, 2]
        hi = mid[t, 1, x] + in2[t, 1, 0] + in2[t, 1, 1] + in2[t, 1, 2]
        (lo, lo_scale), (hi, hi_scale) = coded(lo), coded(hi)

        def put(ref):
            ref[:ROWS, :128] = lo
            ref[:ROWS, 128:] = hi
            ref[ROWS:, :128] = lo_scale
            ref[ROWS:, 128:] = hi_scale

        @pl.when(stays(t))
        def _():
            put(fin.at[zh, lax.rem(t, 4)])

        @pl.when(jnp.logical_not(stays(t)))
        def _():
            put(res.at[t])
            z_copy(t).start()

    def step(s, _):
        @pl.when(s < 8)
        def _():
            @pl.when(s >= 6)
            def _():
                forward(s)

            multiply(s)

            @pl.when(s < 6)
            def _():
                forward(s)

        @pl.when((s >= 1) & (s < 9))
        def _():
            add_cores(s - 1)

        @pl.when((s >= 2) & (s < 10))
        def _():
            add_first(s - 2)

        @pl.when(s >= 3)
        def _():
            add_second(s - 3)

        return 0

    lax.fori_loop(0, 11, step, 0)

    source = 2 * zh + c // 2
    for g in range(2):
        @pl.when(jnp.logical_not((zh == g) & (source == c)))
        def _():
            arrived(fin.at[g], r_z.at[g])
    row_sum = jnp.zeros((ROWS, 128), jnp.float32)
    for k in range(4):
        g = decoded(fin[0, k, :ROWS], fin[0, k, ROWS:]) + decoded(fin[1, k, :ROWS], fin[1, k, ROWS:])
        grad[:, pl.ds(WIDE * k, WIDE)] = g
        sq = g * g + tiny_eps
        row_sum = row_sum + sq[:, :128] + sq[:, 128:]
        col_mine[:, pl.ds(WIDE * k, WIDE)] = jnp.sum(sq, axis=0, keepdims=True)
    row_in[0] = row_sum
    grad_copy = pltpu.make_async_copy(grad, grad_out, s_loc.at[0])
    grad_copy.start()

    def row_copy(j):
        return send(row_in.at[0], row_in.at[j], s_row, r_row, dev(zh, x, y, core, lax.rem(c + j, 4)))

    def col_copy(j):
        return send(col_mine, col_in.at[j - 1], s_col, r_col, plane_peer(j))

    def col_copy2(j):
        q = lax.rem(zh * 2 + core + j, 4)
        return send(col_mid, col_in2.at[j - 1], s_col2, r_col2, dev(q // 2, x, y, q % 2, c))

    def each(lo, hi, f):
        def one(j, _):
            f(j)
            return 0
        lax.fori_loop(lo, hi, one, 0)

    each(1, 16, lambda j: col_copy(j).start())
    each(1, 4, lambda j: row_copy(j).start())
    arrived(col_in, r_col)
    total = col_mine[...]
    for j in range(15):
        total = total + col_in[j]
    col_mid[...] = total
    each(1, 4, lambda j: col_copy2(j).start())
    arrived(row_in.at[pl.ds(1, 3)], r_row)
    rows = jnp.sum(row_in[0] + row_in[1] + row_in[2] + row_in[3], axis=1, keepdims=True)
    eye = lax.broadcasted_iota(jnp.int32, (ROWS, ROWS), 0) == lax.broadcasted_iota(jnp.int32, (ROWS, ROWS), 1)
    rm = jnp.sum(jnp.where(eye, rm_ref[...], 0.0), axis=1, keepdims=True)
    new_row = DECAY * rm + (1.0 - DECAY) * (rows / D)
    nr_ref[...] = jnp.sum(jnp.where(eye, new_row, 0.0), axis=0, keepdims=True)
    arrived(col_in2, r_col2)
    cols = col_mid[...] + col_in2[0] + col_in2[1] + col_in2[2]
    new_col = DECAY * cm_ref[...] + (1.0 - DECAY) * (cols / D)
    nc_ref[...] = new_col
    root_r = 1.0 / jnp.sqrt(new_row)
    root_c = 1.0 / jnp.sqrt(new_col)
    scaled = grad[...] * root_r * root_c
    part = jnp.sum(scaled * scaled)
    row_part = jnp.sum(new_row)
    lane = lax.broadcasted_iota(jnp.int32, (8, 128), 1)
    sca_mine[...] = jnp.where(lane == 0, part, jnp.where(lane == 1, row_part, 0.0))

    def sca_copy(j):
        return send(sca_mine, sca_in.at[j - 1], s_sca, r_sca, plane_peer(j))

    def sca_copy2(j):
        return send(sca_mid, sca_in2.at[j - 1], s_sca2, r_sca2, pole_peer(j))

    each(1, 16, lambda j: sca_copy(j).start())
    arrived(sca_in, r_sca)
    total = sca_mine[...]
    for j in range(15):
        total = total + sca_in[j]
    sca_mid[...] = total
    each(1, 16, lambda j: sca_copy2(j).start())
    arrived(sca_in2, r_sca2)
    total = sca_mid[...]
    for j in range(15):
        total = total + sca_in2[j]
    sum_sq = jnp.sum(jnp.where(lane == 0, total, 0.0), axis=1, keepdims=True)[:1]
    sum_row = jnp.sum(jnp.where(lane == 1, total, 0.0), axis=1, keepdims=True)[:1] / 4.0
    scale_total = sum_row / D
    root_mean = jnp.sqrt(sum_sq * scale_total / (D * D))
    factor = jnp.sqrt(scale_total) / jnp.maximum(1.0, root_mean)
    by_row_ref[...] = jnp.broadcast_to(root_r * factor, (ROWS, 128))
    by_col_ref[...] = root_c

    grad_copy.wait()
    arrived(aa.at[pl.ds(0, 2)], s_a)
    arrived(bb.at[pl.ds(4, 4)], s_b2)

    @pl.when(jnp.logical_not(edge))
    def _():
        arrived(bb.at[pl.ds(0, 4)], s_b1)
        arrived(bb.at[pl.ds(4, 4)], s_fw)

    core_copy(6).wait_send()
    core_copy(7).wait_send()

    def sent(t):
        arrived(in1.at[t], s_1.at[t])
        arrived(in2.at[t], s_2.at[t])

        @pl.when(jnp.logical_not(stays(t)))
        def _():
            z_copy(t).wait_send()

    each(0, 8, sent)
    arrived(row_in.at[pl.ds(1, 3)], s_row)
    arrived(col_in, s_col)
    arrived(col_in2, s_col2)
    arrived(sca_in, s_sca)
    arrived(sca_in2, s_sca2)


def finish(grad_ref, by_row_ref, by_col_ref, w_ref, nr_in, nc_in, nw_ref, up_ref, nr_ref, nc_ref):
    scale = by_row_ref[...]
    for k in range(8):
        at = pl.ds(128 * k, 128)
        update = grad_ref[:, at] * scale * by_col_ref[:, at]
        up_ref[:, at] = update
        nw_ref[:, at] = w_ref[:, at] - learn_rate * update
    nr_ref[...] = nr_in[...]
    nc_ref[...] = nc_in[...]


def body(activations, out_grads, weight, row_moment, col_moment):
    f32, bf16 = jnp.float32, jnp.bfloat16
    V, S = pltpu.VMEM, pltpu.SemaphoreType.DMA
    vmem, hbm = pl.BlockSpec(memory_space=pltpu.VMEM), pl.BlockSpec(memory_space=pl.ANY)
    buffers = [
        V((4, TOK, 512), bf16),
        V((8, TOK, WIDE), bf16),
        V((4, TOK, WIDE), bf16),
        V((STEPS, 2, 4, 4, ROWS, 128), f32),
        V((2, 2, 4, 4, ROWS, 128), f32),
        V((STEPS, 2, 4, 4, ROWS, 128), f32),
        V((STEPS, 2, 4, 4 * ROWS + 16, 128), bf16),
        V((STEPS, 2, 3, 4 * ROWS + 16, 128), bf16),
        V((STEPS, 2, 4, ROWS, 128), f32),
        V((STEPS, 2, 3, ROWS, 128), f32),
        V((STEPS, ROWS + 16, WIDE), bf16),
        V((2, 4, ROWS + 16, WIDE), bf16),
        V((ROWS, FEAT), f32),
        V((4, ROWS, 128), f32),
        V((1, FEAT), f32), V((15, 1, FEAT), f32), V((1, FEAT), f32), V((3, 1, FEAT), f32),
        V((8, 128), f32), V((15, 8, 128), f32), V((8, 128), f32), V((15, 8, 128), f32),
    ]
    sems = [S((6,)), S(()), S(()), S(()), S((4,)), S(()), S((4,)), S((8,)), S(()),
            S((2,)), S((8,)), S((8,)), S((8,)), S((8,)), S((8,)), S(()), S((2,))] + [S(())] * 10
    shape = lambda *dims: jax.ShapeDtypeStruct(dims, f32)
    grad, by_row, by_col, nr, nc = pl.pallas_call(
        kernel,
        out_shape=[shape(ROWS, FEAT), shape(ROWS, 128), shape(1, FEAT), shape(1, ROWS), shape(1, FEAT)],
        in_specs=[hbm, hbm, vmem, vmem],
        out_specs=[hbm, vmem, vmem, vmem, vmem],
        scratch_shapes=buffers + sems,
        compiler_params=pltpu.CompilerParams(
            collective_id=0, has_side_effects=True, vmem_limit_bytes=60 * 2**20
        ),
    )(activations, out_grads, row_moment.reshape(1, ROWS), col_moment.reshape(1, FEAT))
    nw, up, nr, nc = pl.pallas_call(
        finish,
        out_shape=[shape(ROWS, FEAT), shape(ROWS, FEAT), shape(1, ROWS), shape(1, FEAT)],
        in_specs=[vmem] * 6,
        out_specs=[vmem] * 4,
    )(grad, by_row, by_col, weight, nr, nc)
    return nw, up, nr.reshape(ROWS), nc.reshape(FEAT)


def solution(mesh):
    return jax.shard_map(
        body,
        mesh=mesh,
        in_specs=(P("dp", "mp"), P("dp", "mp"), P("dp", "mp"), P("dp"), P("mp")),
        out_specs=(P("dp", "mp"), P("dp", "mp"), P("dp"), P("mp")),
        check_vma=False,
    )
```

```python
import jax
import jax.numpy as jnp
from jax import lax
from jax.experimental import pallas as pl
from jax.experimental.pallas import tpu as pltpu
from jax.sharding import PartitionSpec as P

D = 4096
STEPS_DONE = 10
MESH = pl.DeviceIdType.MESH

learn_rate = 0.01
tiny_eps = 1e-30
DECAY = 1.0 - STEPS_DONE ** (-0.8)

TOK = 768
FEAT = 1024
STEPS = 8
WIDE = 256
ROWS = 64


POWER = 16
TOP = 239.0


def coded(v):
    most = jnp.max(jnp.abs(v), axis=0, keepdims=True)
    scale = (most * 1.01 + 1e-30).astype(jnp.bfloat16)
    u = v * (TOP / scale.astype(jnp.float32))
    m = u * u
    m = m * m
    m = m * m
    m = m * m
    y = jnp.where(u < 0.0, -m, m).astype(jnp.bfloat16)
    return y, jnp.broadcast_to(scale, (16, v.shape[1]))


def decoded(y, scale):
    f = y.astype(jnp.float32)
    m = jnp.exp(jnp.log(jnp.abs(f)) * (1.0 / POWER))
    return jnp.where(f < 0.0, -m, m) * (scale.astype(jnp.float32)[:1] * (1.0 / TOP))


def kernel(
    a_ref, b_ref, rm_ref, cm_ref,
    grad_out, by_row_ref, by_col_ref, nr_ref, nc_ref,
    aa, bb, ps, own, give, take, enc, in1, mid, in2, res, fin, grad,
    row_in, col_mine, col_in, col_mid, col_in2, sca_mine, sca_in, sca_mid, sca_in2,
    s_loc, s_a, r_a, s_b1, r_b1, s_b2, r_b2, r_ps, s_fw,
    s_core, r_core, s_1, r_1, s_2, r_2, s_z, r_z, s_row, s_col, r_row, r_col, s_col2, r_col2, s_sca, r_sca, s_sca2, r_sca2, heard,
):
    d = lax.axis_index("dp")
    c = lax.axis_index("mp")
    zh, x, y, core = d // 32, (d // 8) % 4, (d // 2) % 4, d % 2

    def dev(zh_, x_, y_, core_, c_):
        return (((zh_ * 4 + x_) * 4 + y_) * 2 + core_, c_)

    def plane_peer(j):
        q = lax.rem(x * 4 + y + j, 16)
        return dev(zh, q // 4, q % 4, core, c)

    def pole_peer(j):
        q = lax.rem((zh * 4 + c) * 2 + core + j, 16)
        return dev(q // 8, x, y, q % 2, (q // 2) % 4)

    def send(src, dst, s_sem, r_sem, to):
        return pltpu.make_async_remote_copy(
            src_ref=src, dst_ref=dst, send_sem=s_sem, recv_sem=r_sem, device_id=to, device_id_type=MESH
        )

    def arrived(ref, sem):
        pltpu.make_async_copy(ref, ref, sem).wait()

    up, down = lax.rem(zh * 4 + c + 1, 8), lax.rem(zh * 4 + c + 7, 8)
    neighbours = [
        dev(zh, x, y, 1 - core, c),
        dev(zh, lax.rem(x + 1, 4), y, core, c), dev(zh, lax.rem(x + 3, 4), y, core, c),
        dev(zh, x, lax.rem(y + 1, 4), core, c), dev(zh, x, lax.rem(y + 3, 4), core, c),
        dev(up // 4, x, y, core, up % 4), dev(down // 4, x, y, core, down % 4),
    ]
    barrier = pltpu.get_barrier_semaphore()
    for to in neighbours:
        pl.semaphore_signal(barrier, inc=1, device_id=to, device_id_type=MESH)
    pl.semaphore_wait(barrier, 7)

    def hail(k):
        for to in neighbours:
            pl.semaphore_signal(heard.at[k], inc=1, device_id=to, device_id_type=MESH)
        pl.semaphore_wait(heard.at[k], 7)

    edge = (c == 0) | (c == 3)
    half = lax.rem(c, 2)
    to_pair = dev(zh, x, y, core, c + 1 - 2 * half)
    to_mid = dev(zh, x, y, core, 3 - c)

    def a_copy(i):
        return send(a_ref.at[:, pl.ds(512 * i, 512)], aa.at[2 * half + i], s_a, r_a, to_pair)

    def b1_copy(i):
        return send(b_ref.at[:, pl.ds(WIDE * i, WIDE)], bb.at[i], s_b1, r_b1.at[i], to_mid)

    def b_piece(i):
        return b_ref.at[:, pl.ds(128 * i, 128)]

    def bb_piece(i):
        return bb.at[4 + i // 2, :, pl.ds(128 * (i % 2), 128)]

    def ps_piece(i):
        return ps.at[i // 2, :, pl.ds(128 * (i % 2), 128)]

    def b2_copy(i):
        return send(b_piece(i), bb_piece(i), s_b2, r_b2.at[i // 2], to_pair)

    def ps_copy(i):
        return send(b_piece(i), ps_piece(i), s_b2, r_ps.at[i], to_pair)

    def fw_copy(i):
        return send(ps_piece(i), bb_piece(i), s_fw, r_b2.at[i // 2], to_mid)

    @pl.when(edge)
    def _():
        for i in range(2):
            a_copy(i).start()
        for i in range(8):
            ps_copy(i).start()

    @pl.when(jnp.logical_not(edge))
    def _():
        for i in range(2):
            a_copy(i).start()
            b1_copy(2 * i).start()
            b1_copy(2 * i + 1).start()
        for i in range(8):
            b2_copy(i).start()

    def a_local(i):
        return pltpu.make_async_copy(a_ref.at[:, pl.ds(512 * i, 512)], aa.at[2 * half + i], s_loc.at[i])

    def b_local(i):
        return pltpu.make_async_copy(b_ref.at[:, pl.ds(WIDE * i, WIDE)], bb.at[i], s_loc.at[2 + i])

    for i in range(2):
        a_local(i).start()

    @pl.when(edge)
    def _():
        for i in range(4):
            b_local(i).start()

    for k in range(4):
        hail(k)

    @pl.when(edge)
    def _():
        for i in range(4):
            b_local(i).wait()

    for i in range(2):
        a_local(i).wait()
    arrived(aa.at[pl.ds(0, 2)], r_a)

    def forward(i):
        @pl.when(jnp.logical_not(edge))
        def _():
            for k in range(8):
                @pl.when(i == k)
                def _():
                    ps_copy(k).wait_recv()
                    fw_copy(k).start()

    def core_copy(t):
        return send(give.at[t % 2], take.at[t], s_core.at[t % 2], r_core.at[t], dev(zh, x, y, 1 - core, c))

    def multiply(t):
        @pl.when((t < 4) & jnp.logical_not(edge))
        def _():
            for k in range(4):
                @pl.when(t == k)
                def _():
                    b1_copy(k).wait_recv()

        for k in range(4, 8):
            @pl.when(t == k)
            def _():
                arrived(bb.at[k], r_b2.at[k - 4])

        @pl.when(t >= 2)
        def _():
            core_copy(t - 2).wait_send()

        def of_x(xx, _):
            r = lax.dot_general(
                aa[xx], bb[t], (((0,), (0,)), ((), ())), preferred_element_type=jnp.float32
            )
            for yy in range(4):
                lo, hi = r[128 * yy : 128 * yy + 64], r[128 * yy + 64 : 128 * yy + 128]
                keep, go = jnp.where(core == 0, lo, hi), jnp.where(core == 0, hi, lo)
                own[t, 0, xx, yy] = keep[:, :128]
                own[t, 1, yy, xx] = keep[:, 128:]
                give[t % 2, 0, xx, yy] = go[:, :128]
                give[t % 2, 1, yy, xx] = go[:, 128:]
            return 0

        lax.fori_loop(0, 4, of_x, 0)
        core_copy(t).start()

    def copies_1(t):
        out = []
        for j in range(1, 4):
            out.append(send(enc.at[t, 0, lax.rem(x + j, 4)], in1.at[t, 0, j - 1], s_1.at[t], r_1.at[t],
                            dev(zh, lax.rem(x + j, 4), y, core, c)))
            out.append(send(enc.at[t, 1, lax.rem(y + j, 4)], in1.at[t, 1, j - 1], s_1.at[t], r_1.at[t],
                            dev(zh, x, lax.rem(y + j, 4), core, c)))
        return out

    def add_cores(t):
        core_copy(t).wait_recv()

        def of(k, _):
            v = own[t, k // 4, k % 4] + take[t, k // 4, k % 4]
            own[t, k // 4, k % 4] = v
            code, scale = coded(v.reshape(4 * ROWS, 128))
            enc[t, k // 4, k % 4, : 4 * ROWS] = code
            enc[t, k // 4, k % 4, 4 * ROWS :] = scale
            return 0

        lax.fori_loop(0, 8, of, 0)
        for q in copies_1(t):
            q.start()

    def copies_2(t):
        out = []
        for j in range(1, 4):
            out.append(send(mid.at[t, 0, lax.rem(y + j, 4)], in2.at[t, 0, j - 1], s_2.at[t], r_2.at[t], dev(zh, x, lax.rem(y + j, 4), core, c)))
            out.append(send(mid.at[t, 1, lax.rem(x + j, 4)], in2.at[t, 1, j - 1], s_2.at[t], r_2.at[t], dev(zh, lax.rem(x + j, 4), y, core, c)))
        return out

    def add_first(t):
        arrived(in1.at[t], r_1.at[t])

        def of(h, _):
            total = own[t, h, jnp.where(h == 0, x, y)].reshape(4 * ROWS, 128)
            for k in range(3):
                total = total + decoded(in1[t, h, k, : 4 * ROWS], in1[t, h, k, 4 * ROWS :])
            mid[t, h] = total.reshape(4, ROWS, 128)
            return 0

        lax.fori_loop(0, 2, of, 0)
        for q in copies_2(t):
            q.start()

    def target(t):
        return jnp.where(t < 4, jnp.where(edge, c, 3 - c), lax.rem(2 * c + 1, 5))

    def stays(t):
        return (zh == c // 2) & (target(t) == c)

    def z_copy(t):
        return send(res.at[t], fin.at[zh, lax.rem(t, 4)], s_z, r_z.at[zh],
                    dev(c // 2, x, y, core, target(t)))

    def add_second(t):
        arrived(in2.at[t], r_2.at[t])
        lo = mid[t, 0, y] + in2[t, 0, 0] + in2[t, 0, 1] + in2[t, 0, 2]
        hi = mid[t, 1, x] + in2[t, 1, 0] + in2[t, 1, 1] + in2[t, 1, 2]
        (lo, lo_scale), (hi, hi_scale) = coded(lo), coded(hi)

        def put(ref):
            ref[:ROWS, :128] = lo
            ref[:ROWS, 128:] = hi
            ref[ROWS:, :128] = lo_scale
            ref[ROWS:, 128:] = hi_scale

        @pl.when(stays(t))
        def _():
            put(fin.at[zh, lax.rem(t, 4)])

        @pl.when(jnp.logical_not(stays(t)))
        def _():
            put(res.at[t])
            z_copy(t).start()

    def step(s, _):
        @pl.when(s < 8)
        def _():
            @pl.when(s >= 6)
            def _():
                forward(s)

            multiply(s)

            @pl.when(s < 6)
            def _():
                forward(s)

        @pl.when((s >= 1) & (s < 9))
        def _():
            add_cores(s - 1)

        @pl.when((s >= 2) & (s < 10))
        def _():
            add_first(s - 2)

        @pl.when(s >= 3)
        def _():
            add_second(s - 3)

        return 0

    lax.fori_loop(0, 11, step, 0)

    source = 2 * zh + c // 2
    for g in range(2):
        @pl.when(jnp.logical_not((zh == g) & (source == c)))
        def _():
            arrived(fin.at[g], r_z.at[g])
    row_sum = jnp.zeros((ROWS, 128), jnp.float32)
    for k in range(4):
        g = decoded(fin[0, k, :ROWS], fin[0, k, ROWS:]) + decoded(fin[1, k, :ROWS], fin[1, k, ROWS:])
        grad[:, pl.ds(WIDE * k, WIDE)] = g
        sq = g * g + tiny_eps
        row_sum = row_sum + sq[:, :128] + sq[:, 128:]
        col_mine[:, pl.ds(WIDE * k, WIDE)] = jnp.sum(sq, axis=0, keepdims=True)
    row_in[0] = row_sum
    grad_copy = pltpu.make_async_copy(grad, grad_out, s_loc.at[0])
    grad_copy.start()

    def row_copy(j):
        return send(row_in.at[0], row_in.at[j], s_row, r_row, dev(zh, x, y, core, lax.rem(c + j, 4)))

    def col_copy(j):
        return send(col_mine, col_in.at[j - 1], s_col, r_col, plane_peer(j))

    def col_copy2(j):
        q = lax.rem(zh * 2 + core + j, 4)
        return send(col_mid, col_in2.at[j - 1], s_col2, r_col2, dev(q // 2, x, y, q % 2, c))

    def each(lo, hi, f):
        def one(j, _):
            f(j)
            return 0
        lax.fori_loop(lo, hi, one, 0)

    each(1, 4, lambda j: row_copy(j).start())
    each(1, 16, lambda j: col_copy(j).start())
    eye = lax.broadcasted_iota(jnp.int32, (ROWS, ROWS), 0) == lax.broadcasted_iota(jnp.int32, (ROWS, ROWS), 1)
    rm = jnp.sum(jnp.where(eye, rm_ref[...], 0.0), axis=1, keepdims=True)
    arrived(row_in.at[pl.ds(1, 3)], r_row)
    rows = jnp.sum(row_in[0] + row_in[1] + row_in[2] + row_in[3], axis=1, keepdims=True)
    new_row = DECAY * rm + (1.0 - DECAY) * (rows / D)
    inverse = 1.0 / new_row
    for k in range(4):
        g = grad[:, pl.ds(WIDE * k, WIDE)]
        sca_mine[:, pl.ds(WIDE * k, WIDE)] = jnp.sum(g * g * inverse, axis=0, keepdims=True)
    sca_mine[:, FEAT:] = jnp.broadcast_to(jnp.sum(new_row, axis=0, keepdims=True), (1, 128))

    def sca_copy(j):
        return send(sca_mine, sca_in.at[j - 1], s_sca, r_sca, plane_peer(j))

    def sca_copy2(j):
        return send(sca_mid, sca_in2.at[j - 1], s_sca2, r_sca2, pole_peer(j))

    arrived(col_in, r_col)
    total = col_mine[...]
    for j in range(15):
        total = total + col_in[j]
    col_mid[...] = total
    each(1, 4, lambda j: col_copy2(j).start())
    each(1, 16, lambda j: sca_copy(j).start())
    nr_ref[...] = jnp.sum(jnp.where(eye, new_row, 0.0), axis=0, keepdims=True)
    root_r = 1.0 / jnp.sqrt(new_row)
    arrived(col_in2, r_col2)
    cols = col_mid[...] + col_in2[0] + col_in2[1] + col_in2[2]
    new_col = DECAY * cm_ref[...] + (1.0 - DECAY) * (cols / D)
    nc_ref[...] = new_col
    root_c = 1.0 / jnp.sqrt(new_col)
    by_col_ref[...] = root_c
    inverse = 1.0 / new_col
    arrived(sca_in, r_sca)
    total = sca_mine[...]
    for j in range(15):
        total = total + sca_in[j]
    part = jnp.sum(total[:, :FEAT] * inverse, axis=1, keepdims=True)
    lane = lax.broadcasted_iota(jnp.int32, (8, 128), 1)
    sca_mid[...] = jnp.where(lane == 0, part, jnp.where(lane == 1, total[:, FEAT:], 0.0))
    each(1, 16, lambda j: sca_copy2(j).start())
    arrived(sca_in2, r_sca2)
    total = sca_mid[...]
    for j in range(15):
        total = total + sca_in2[j]
    sum_sq = jnp.sum(jnp.where(lane == 0, total, 0.0), axis=1, keepdims=True)[:1]
    sum_row = jnp.sum(jnp.where(lane == 1, total, 0.0), axis=1, keepdims=True)[:1] / 4.0
    scale_total = sum_row / D
    root_mean = jnp.sqrt(sum_sq * scale_total / (D * D))
    factor = jnp.sqrt(scale_total) / jnp.maximum(1.0, root_mean)
    by_row_ref[...] = jnp.broadcast_to(root_r * factor, (ROWS, 128))

    grad_copy.wait()
    arrived(aa.at[pl.ds(0, 2)], s_a)
    arrived(bb.at[pl.ds(4, 4)], s_b2)

    @pl.when(jnp.logical_not(edge))
    def _():
        arrived(bb.at[pl.ds(0, 4)], s_b1)
        arrived(bb.at[pl.ds(4, 4)], s_fw)

    core_copy(6).wait_send()
    core_copy(7).wait_send()

    def sent(t):
        arrived(in1.at[t], s_1.at[t])
        arrived(in2.at[t], s_2.at[t])

        @pl.when(jnp.logical_not(stays(t)))
        def _():
            z_copy(t).wait_send()

    each(0, 8, sent)
    arrived(row_in.at[pl.ds(1, 3)], s_row)
    arrived(col_in, s_col)
    arrived(col_in2, s_col2)
    arrived(sca_in, s_sca)
    arrived(sca_in2, s_sca2)


def finish(grad_ref, by_row_ref, by_col_ref, w_ref, nr_in, nc_in, nw_ref, up_ref, nr_ref, nc_ref):
    scale = by_row_ref[...]
    for k in range(8):
        at = pl.ds(128 * k, 128)
        update = grad_ref[:, at] * scale * by_col_ref[:, at]
        up_ref[:, at] = update
        nw_ref[:, at] = w_ref[:, at] - learn_rate * update
    nr_ref[...] = nr_in[...]
    nc_ref[...] = nc_in[...]


def body(activations, out_grads, weight, row_moment, col_moment):
    f32, bf16 = jnp.float32, jnp.bfloat16
    V, S = pltpu.VMEM, pltpu.SemaphoreType.DMA
    vmem, hbm = pl.BlockSpec(memory_space=pltpu.VMEM), pl.BlockSpec(memory_space=pl.ANY)
    buffers = [
        V((4, TOK, 512), bf16),
        V((8, TOK, WIDE), bf16),
        V((4, TOK, WIDE), bf16),
        V((STEPS, 2, 4, 4, ROWS, 128), f32),
        V((2, 2, 4, 4, ROWS, 128), f32),
        V((STEPS, 2, 4, 4, ROWS, 128), f32),
        V((STEPS, 2, 4, 4 * ROWS + 16, 128), bf16),
        V((STEPS, 2, 3, 4 * ROWS + 16, 128), bf16),
        V((STEPS, 2, 4, ROWS, 128), f32),
        V((STEPS, 2, 3, ROWS, 128), f32),
        V((STEPS, ROWS + 16, WIDE), bf16),
        V((2, 4, ROWS + 16, WIDE), bf16),
        V((ROWS, FEAT), f32),
        V((4, ROWS, 128), f32),
        V((1, FEAT), f32), V((15, 1, FEAT), f32), V((1, FEAT), f32), V((3, 1, FEAT), f32),
        V((1, FEAT + 128), f32), V((15, 1, FEAT + 128), f32), V((8, 128), f32), V((15, 8, 128), f32),
    ]
    sems = [S((6,)), S(()), S(()), S(()), S((4,)), S(()), S((4,)), S((8,)), S(()),
            S((2,)), S((8,)), S((8,)), S((8,)), S((8,)), S((8,)), S(()), S((2,))] + [S(())] * 10 + [pltpu.SemaphoreType.REGULAR((4,))]
    shape = lambda *dims: jax.ShapeDtypeStruct(dims, f32)
    grad, by_row, by_col, nr, nc = pl.pallas_call(
        kernel,
        out_shape=[shape(ROWS, FEAT), shape(ROWS, 128), shape(1, FEAT), shape(1, ROWS), shape(1, FEAT)],
        in_specs=[hbm, hbm, vmem, vmem],
        out_specs=[hbm, vmem, vmem, vmem, vmem],
        scratch_shapes=buffers + sems,
        compiler_params=pltpu.CompilerParams(
            collective_id=0, has_side_effects=True, vmem_limit_bytes=60 * 2**20
        ),
    )(activations, out_grads, row_moment.reshape(1, ROWS), col_moment.reshape(1, FEAT))
    nw, up, nr, nc = pl.pallas_call(
        finish,
        out_shape=[shape(ROWS, FEAT), shape(ROWS, FEAT), shape(1, ROWS), shape(1, FEAT)],
        in_specs=[vmem] * 6,
        out_specs=[vmem] * 4,
    )(grad, by_row, by_col, weight, nr, nc)
    return nw, up, nr.reshape(ROWS), nc.reshape(FEAT)


def solution(mesh):
    return jax.shard_map(
        body,
        mesh=mesh,
        in_specs=(P("dp", "mp"), P("dp", "mp"), P("dp", "mp"), P("dp"), P("mp")),
        out_specs=(P("dp", "mp"), P("dp", "mp"), P("dp"), P("mp")),
        check_vma=False,
    )
```

```python
import jax
import jax.numpy as jnp
from jax import lax
from jax.experimental import pallas as pl
from jax.experimental.pallas import tpu as pltpu
from jax.sharding import PartitionSpec as P

D = 4096
STEPS_DONE = 10
MESH = pl.DeviceIdType.MESH

learn_rate = 0.01
tiny_eps = 1e-30
DECAY = 1.0 - STEPS_DONE ** (-0.8)

TOK = 768
FEAT = 1024
STEPS = 8
WIDE = 256
ROWS = 64


POWER = 16
TOP = 239.0


def coded(v):
    most = jnp.max(jnp.abs(v), axis=0, keepdims=True)
    scale = (most * 1.01 + 1e-30).astype(jnp.bfloat16)
    u = v * (TOP / scale.astype(jnp.float32))
    m = u * u
    m = m * m
    m = m * m
    m = m * m
    y = jnp.where(u < 0.0, -m, m).astype(jnp.bfloat16)
    return y, jnp.broadcast_to(scale, (16, v.shape[1]))


def decoded(y, scale):
    f = y.astype(jnp.float32)
    m = jnp.exp(jnp.log(jnp.abs(f)) * (1.0 / POWER))
    return jnp.where(f < 0.0, -m, m) * (scale.astype(jnp.float32)[:1] * (1.0 / TOP))


def kernel(
    a_ref, b_ref, rm_ref, cm_ref,
    grad_out, by_row_ref, by_col_ref, nr_ref, nc_ref,
    aa, bb, ps, own, give, take, enc, in1, mid, in2, res, fin, grad,
    row_in, col_mine, col_in, col_mid, col_in2, sca_mine, sca_in, sca_mid, sca_in2,
    s_loc, s_a, r_a, s_b1, r_b1, s_b2, r_b2, r_ps, s_fw,
    s_core, r_core, s_1, r_1, s_2, r_2, s_z, r_z, s_row, s_col, r_row, r_col, s_col2, r_col2, s_sca, r_sca, s_sca2, r_sca2, heard,
):
    d = lax.axis_index("dp")
    c = lax.axis_index("mp")
    zh, x, y, core = d // 32, (d // 8) % 4, (d // 2) % 4, d % 2

    def dev(zh_, x_, y_, core_, c_):
        return (((zh_ * 4 + x_) * 4 + y_) * 2 + core_, c_)

    def plane_peer(j):
        q = lax.rem(x * 4 + y + j, 16)
        return dev(zh, q // 4, q % 4, core, c)

    def pole_peer(j):
        q = lax.rem((zh * 4 + c) * 2 + core + j, 16)
        return dev(q // 8, x, y, q % 2, (q // 2) % 4)

    def send(src, dst, s_sem, r_sem, to):
        return pltpu.make_async_remote_copy(
            src_ref=src, dst_ref=dst, send_sem=s_sem, recv_sem=r_sem, device_id=to, device_id_type=MESH
        )

    def arrived(ref, sem):
        pltpu.make_async_copy(ref, ref, sem).wait()

    up, down = lax.rem(zh * 4 + c + 1, 8), lax.rem(zh * 4 + c + 7, 8)
    neighbours = [
        dev(zh, x, y, 1 - core, c),
        dev(zh, lax.rem(x + 1, 4), y, core, c), dev(zh, lax.rem(x + 3, 4), y, core, c),
        dev(zh, x, lax.rem(y + 1, 4), core, c), dev(zh, x, lax.rem(y + 3, 4), core, c),
        dev(up // 4, x, y, core, up % 4), dev(down // 4, x, y, core, down % 4),
    ]
    barrier = pltpu.get_barrier_semaphore()
    for to in neighbours:
        pl.semaphore_signal(barrier, inc=1, device_id=to, device_id_type=MESH)
    pl.semaphore_wait(barrier, 7)

    def hail(k):
        for to in neighbours:
            pl.semaphore_signal(heard.at[k], inc=1, device_id=to, device_id_type=MESH)
        pl.semaphore_wait(heard.at[k], 7)

    edge = (c == 0) | (c == 3)
    half = lax.rem(c, 2)
    to_pair = dev(zh, x, y, core, c + 1 - 2 * half)
    to_mid = dev(zh, x, y, core, 3 - c)

    def a_copy(i):
        return send(a_ref.at[:, pl.ds(512 * i, 512)], aa.at[2 * half + i], s_a, r_a, to_pair)

    def b1_copy(i):
        return send(b_ref.at[:, pl.ds(WIDE * i, WIDE)], bb.at[i], s_b1, r_b1.at[i], to_mid)

    def piece(i):
        return pl.ds(192 * (i % 4), 192)

    def b_piece(i):
        return b_ref.at[piece(i), pl.ds(WIDE * (i // 4), WIDE)]

    def bb_piece(i):
        return bb.at[4 + i // 4, piece(i)]

    def ps_piece(i):
        return ps.at[i // 4, piece(i)]

    def b2_copy(i):
        return send(b_piece(i), bb_piece(i), s_b2, r_b2.at[i // 4], to_pair)

    def ps_copy(i):
        return send(b_piece(i), ps_piece(i), s_b2, r_ps.at[i], to_pair)

    def fw_copy(i):
        return send(ps_piece(i), bb_piece(i), s_fw, r_b2.at[i // 4], to_mid)

    @pl.when(edge)
    def _():
        for i in range(2):
            a_copy(i).start()
        for i in range(16):
            ps_copy(i).start()

    @pl.when(jnp.logical_not(edge))
    def _():
        for i in range(2):
            a_copy(i).start()
            b1_copy(2 * i).start()
            b1_copy(2 * i + 1).start()
        for i in range(16):
            b2_copy(i).start()

    def a_local(i):
        return pltpu.make_async_copy(a_ref.at[:, pl.ds(512 * i, 512)], aa.at[2 * half + i], s_loc.at[i])

    def b_local(i):
        return pltpu.make_async_copy(b_ref.at[:, pl.ds(WIDE * i, WIDE)], bb.at[i], s_loc.at[2 + i])

    for i in range(2):
        a_local(i).start()

    @pl.when(edge)
    def _():
        for i in range(4):
            b_local(i).start()

    for k in range(4):
        hail(k)

    @pl.when(edge)
    def _():
        for i in range(4):
            b_local(i).wait()

    for i in range(2):
        a_local(i).wait()
    arrived(aa.at[pl.ds(0, 2)], r_a)

    def forward(s, pieces):
        @pl.when(jnp.logical_not(edge))
        def _():
            for at, k in pieces:
                @pl.when(s == at)
                def _():
                    ps_copy(k).wait_recv()
                    fw_copy(k).start()

    def core_copy(t):
        return send(give.at[t % 2], take.at[t], s_core.at[t % 2], r_core.at[t], dev(zh, x, y, 1 - core, c))

    def multiply(t):
        @pl.when((t < 4) & jnp.logical_not(edge))
        def _():
            for k in range(4):
                @pl.when(t == k)
                def _():
                    b1_copy(k).wait_recv()

        for k in range(4, 8):
            @pl.when(t == k)
            def _():
                arrived(bb.at[k], r_b2.at[k - 4])

        @pl.when(t >= 2)
        def _():
            core_copy(t - 2).wait_send()

        def of_x(xx, _):
            r = lax.dot_general(
                aa[xx], bb[t], (((0,), (0,)), ((), ())), preferred_element_type=jnp.float32
            )
            for yy in range(4):
                lo, hi = r[128 * yy : 128 * yy + 64], r[128 * yy + 64 : 128 * yy + 128]
                keep, go = jnp.where(core == 0, lo, hi), jnp.where(core == 0, hi, lo)
                own[t, 0, xx, yy] = keep[:, :128]
                own[t, 1, yy, xx] = keep[:, 128:]
                give[t % 2, 0, xx, yy] = go[:, :128]
                give[t % 2, 1, yy, xx] = go[:, 128:]
            return 0

        lax.fori_loop(0, 4, of_x, 0)
        core_copy(t).start()

    def copies_1(t):
        out = []
        for j in range(1, 4):
            out.append(send(enc.at[t, 0, lax.rem(x + j, 4)], in1.at[t, 0, j - 1], s_1.at[t], r_1.at[t],
                            dev(zh, lax.rem(x + j, 4), y, core, c)))
            out.append(send(enc.at[t, 1, lax.rem(y + j, 4)], in1.at[t, 1, j - 1], s_1.at[t], r_1.at[t],
                            dev(zh, x, lax.rem(y + j, 4), core, c)))
        return out

    def add_cores(t):
        core_copy(t).wait_recv()

        def of(k, _):
            h, q = k // 4, k % 4
            v = own[t, h, q] + take[t, h, q]
            mine = q == jnp.where(h == 0, x, y)

            @pl.when(mine)
            def _():
                own[t, h, q] = v

            @pl.when(jnp.logical_not(mine))
            def _():
                code, scale = coded(v.reshape(4 * ROWS, 128))
                enc[t, h, q, : 4 * ROWS] = code
                enc[t, h, q, 4 * ROWS :] = scale

            return 0

        lax.fori_loop(0, 8, of, 0)
        for q in copies_1(t):
            q.start()

    def copies_2(t):
        out = []
        for j in range(1, 4):
            out.append(send(mid.at[t, 0, lax.rem(y + j, 4)], in2.at[t, 0, j - 1], s_2.at[t], r_2.at[t], dev(zh, x, lax.rem(y + j, 4), core, c)))
            out.append(send(mid.at[t, 1, lax.rem(x + j, 4)], in2.at[t, 1, j - 1], s_2.at[t], r_2.at[t], dev(zh, lax.rem(x + j, 4), y, core, c)))
        return out

    def add_first(t):
        arrived(in1.at[t], r_1.at[t])

        def of(h, _):
            total = own[t, h, jnp.where(h == 0, x, y)].reshape(4 * ROWS, 128)
            for k in range(3):
                total = total + decoded(in1[t, h, k, : 4 * ROWS], in1[t, h, k, 4 * ROWS :])
            mid[t, h] = total.reshape(4, ROWS, 128)
            return 0

        lax.fori_loop(0, 2, of, 0)
        for q in copies_2(t):
            q.start()

    def target(t):
        return jnp.where(t < 4, jnp.where(edge, c, 3 - c), lax.rem(2 * c + 1, 5))

    def stays(t):
        return (zh == c // 2) & (target(t) == c)

    def z_copy(t):
        return send(res.at[t], fin.at[zh, lax.rem(t, 4)], s_z, r_z.at[zh],
                    dev(c // 2, x, y, core, target(t)))

    def add_second(t):
        arrived(in2.at[t], r_2.at[t])
        lo = mid[t, 0, y] + in2[t, 0, 0] + in2[t, 0, 1] + in2[t, 0, 2]
        hi = mid[t, 1, x] + in2[t, 1, 0] + in2[t, 1, 1] + in2[t, 1, 2]
        (lo, lo_scale), (hi, hi_scale) = coded(lo), coded(hi)

        def put(ref):
            ref[:ROWS, :128] = lo
            ref[:ROWS, 128:] = hi
            ref[ROWS:, :128] = lo_scale
            ref[ROWS:, 128:] = hi_scale

        @pl.when(stays(t))
        def _():
            put(fin.at[zh, lax.rem(t, 4)])

        @pl.when(jnp.logical_not(stays(t)))
        def _():
            put(res.at[t])
            z_copy(t).start()

    def when(cond, f, t):
        @pl.when(cond)
        def _():
            f(t)

    def step(s, _):
        forward(s, [(6, 12), (6, 13), (7, 14), (7, 15)])
        when(s < 8, multiply, s)
        forward(s, [(k, 2 * k) for k in range(6)])
        when((s >= 1) & (s < 9), add_cores, s - 1)
        forward(s, [(k, 2 * k + 1) for k in range(6)])
        when((s >= 3) & (s < 11), add_first, s - 3)
        when(s >= 5, add_second, s - 5)
        return 0

    lax.fori_loop(0, 13, step, 0)

    source = 2 * zh + c // 2
    for g in range(2):
        @pl.when(jnp.logical_not((zh == g) & (source == c)))
        def _():
            arrived(fin.at[g], r_z.at[g])
    row_sum = jnp.zeros((ROWS, 128), jnp.float32)
    for k in range(4):
        g = decoded(fin[0, k, :ROWS], fin[0, k, ROWS:]) + decoded(fin[1, k, :ROWS], fin[1, k, ROWS:])
        grad[:, pl.ds(WIDE * k, WIDE)] = g
        sq = g * g + tiny_eps
        row_sum = row_sum + sq[:, :128] + sq[:, 128:]
        col_mine[:, pl.ds(WIDE * k, WIDE)] = jnp.sum(sq, axis=0, keepdims=True)
    row_in[0] = row_sum
    grad_copy = pltpu.make_async_copy(grad, grad_out, s_loc.at[0])
    grad_copy.start()

    def row_copy(j):
        return send(row_in.at[0], row_in.at[j], s_row, r_row, dev(zh, x, y, core, lax.rem(c + j, 4)))

    def col_copy(j):
        return send(col_mine, col_in.at[j - 1], s_col, r_col, plane_peer(j))

    def col_copy2(j):
        q = lax.rem(zh * 2 + core + j, 4)
        return send(col_mid, col_in2.at[j - 1], s_col2, r_col2, dev(q // 2, x, y, q % 2, c))

    def each(lo, hi, f):
        def one(j, _):
            f(j)
            return 0
        lax.fori_loop(lo, hi, one, 0)

    each(1, 4, lambda j: row_copy(j).start())
    each(1, 16, lambda j: col_copy(j).start())
    eye = lax.broadcasted_iota(jnp.int32, (ROWS, ROWS), 0) == lax.broadcasted_iota(jnp.int32, (ROWS, ROWS), 1)
    rm = jnp.sum(jnp.where(eye, rm_ref[...], 0.0), axis=1, keepdims=True)
    arrived(row_in.at[pl.ds(1, 3)], r_row)
    rows = jnp.sum(row_in[0] + row_in[1] + row_in[2] + row_in[3], axis=1, keepdims=True)
    new_row = DECAY * rm + (1.0 - DECAY) * (rows / D)
    inverse = 1.0 / new_row
    for k in range(4):
        g = grad[:, pl.ds(WIDE * k, WIDE)]
        sca_mine[:, pl.ds(WIDE * k, WIDE)] = jnp.sum(g * g * inverse, axis=0, keepdims=True)
    sca_mine[:, FEAT:] = jnp.broadcast_to(jnp.sum(new_row, axis=0, keepdims=True), (1, 128))

    def sca_copy(j):
        return send(sca_mine, sca_in.at[j - 1], s_sca, r_sca, plane_peer(j))

    def sca_copy2(j):
        return send(sca_mid, sca_in2.at[j - 1], s_sca2, r_sca2, pole_peer(j))

    arrived(col_in, r_col)
    total = col_mine[...]
    for j in range(15):
        total = total + col_in[j]
    col_mid[...] = total
    each(1, 4, lambda j: col_copy2(j).start())
    each(1, 16, lambda j: sca_copy(j).start())
    nr_ref[...] = jnp.sum(jnp.where(eye, new_row, 0.0), axis=0, keepdims=True)
    root_r = 1.0 / jnp.sqrt(new_row)
    arrived(col_in2, r_col2)
    cols = col_mid[...] + col_in2[0] + col_in2[1] + col_in2[2]
    new_col = DECAY * cm_ref[...] + (1.0 - DECAY) * (cols / D)
    nc_ref[...] = new_col
    root_c = 1.0 / jnp.sqrt(new_col)
    by_col_ref[...] = root_c
    inverse = 1.0 / new_col
    arrived(sca_in, r_sca)
    total = sca_mine[...]
    for j in range(15):
        total = total + sca_in[j]
    part = jnp.sum(total[:, :FEAT] * inverse, axis=1, keepdims=True)
    lane = lax.broadcasted_iota(jnp.int32, (8, 128), 1)
    sca_mid[...] = jnp.where(lane == 0, part, jnp.where(lane == 1, total[:, FEAT:], 0.0))
    each(1, 16, lambda j: sca_copy2(j).start())
    arrived(sca_in2, r_sca2)
    total = sca_mid[...]
    for j in range(15):
        total = total + sca_in2[j]
    sum_sq = jnp.sum(jnp.where(lane == 0, total, 0.0), axis=1, keepdims=True)[:1]
    sum_row = jnp.sum(jnp.where(lane == 1, total, 0.0), axis=1, keepdims=True)[:1] / 4.0
    scale_total = sum_row / D
    root_mean = jnp.sqrt(sum_sq * scale_total / (D * D))
    factor = jnp.sqrt(scale_total) / jnp.maximum(1.0, root_mean)
    by_row_ref[...] = jnp.broadcast_to(root_r * factor, (ROWS, 128))

    grad_copy.wait()
    arrived(aa.at[pl.ds(0, 2)], s_a)
    arrived(bb.at[pl.ds(4, 4)], s_b2)

    @pl.when(jnp.logical_not(edge))
    def _():
        arrived(bb.at[pl.ds(0, 4)], s_b1)
        arrived(bb.at[pl.ds(4, 4)], s_fw)

    core_copy(6).wait_send()
    core_copy(7).wait_send()

    def sent(t):
        arrived(in1.at[t], s_1.at[t])
        arrived(in2.at[t], s_2.at[t])

        @pl.when(jnp.logical_not(stays(t)))
        def _():
            z_copy(t).wait_send()

    each(0, 8, sent)
    arrived(row_in.at[pl.ds(1, 3)], s_row)
    arrived(col_in, s_col)
    arrived(col_in2, s_col2)
    arrived(sca_in, s_sca)
    arrived(sca_in2, s_sca2)


def finish(grad_ref, by_row_ref, by_col_ref, w_ref, nr_in, nc_in, nw_ref, up_ref, nr_ref, nc_ref):
    scale = by_row_ref[...]
    for k in range(8):
        at = pl.ds(128 * k, 128)
        update = grad_ref[:, at] * scale * by_col_ref[:, at]
        up_ref[:, at] = update
        nw_ref[:, at] = w_ref[:, at] - learn_rate * update
    nr_ref[...] = nr_in[...]
    nc_ref[...] = nc_in[...]


def body(activations, out_grads, weight, row_moment, col_moment):
    f32, bf16 = jnp.float32, jnp.bfloat16
    V, S = pltpu.VMEM, pltpu.SemaphoreType.DMA
    vmem, hbm = pl.BlockSpec(memory_space=pltpu.VMEM), pl.BlockSpec(memory_space=pl.ANY)
    buffers = [
        V((4, TOK, 512), bf16),
        V((8, TOK, WIDE), bf16),
        V((4, TOK, WIDE), bf16),
        V((STEPS, 2, 4, 4, ROWS, 128), f32),
        V((2, 2, 4, 4, ROWS, 128), f32),
        V((STEPS, 2, 4, 4, ROWS, 128), f32),
        V((STEPS, 2, 4, 4 * ROWS + 16, 128), bf16),
        V((STEPS, 2, 3, 4 * ROWS + 16, 128), bf16),
        V((STEPS, 2, 4, ROWS, 128), f32),
        V((STEPS, 2, 3, ROWS, 128), f32),
        V((STEPS, ROWS + 16, WIDE), bf16),
        V((2, 4, ROWS + 16, WIDE), bf16),
        V((ROWS, FEAT), f32),
        V((4, ROWS, 128), f32),
        V((1, FEAT), f32), V((15, 1, FEAT), f32), V((1, FEAT), f32), V((3, 1, FEAT), f32),
        V((1, FEAT + 128), f32), V((15, 1, FEAT + 128), f32), V((8, 128), f32), V((15, 8, 128), f32),
    ]
    sems = [S((6,)), S(()), S(()), S(()), S((4,)), S(()), S((4,)), S((16,)), S(()),
            S((2,)), S((8,)), S((8,)), S((8,)), S((8,)), S((8,)), S(()), S((2,))] + [S(())] * 10 + [pltpu.SemaphoreType.REGULAR((4,))]
    shape = lambda *dims: jax.ShapeDtypeStruct(dims, f32)
    grad, by_row, by_col, nr, nc = pl.pallas_call(
        kernel,
        out_shape=[shape(ROWS, FEAT), shape(ROWS, 128), shape(1, FEAT), shape(1, ROWS), shape(1, FEAT)],
        in_specs=[hbm, hbm, vmem, vmem],
        out_specs=[hbm, vmem, vmem, vmem, vmem],
        scratch_shapes=buffers + sems,
        compiler_params=pltpu.CompilerParams(
            collective_id=0, has_side_effects=True, vmem_limit_bytes=60 * 2**20
        ),
    )(activations, out_grads, row_moment.reshape(1, ROWS), col_moment.reshape(1, FEAT))
    nw, up, nr, nc = pl.pallas_call(
        finish,
        out_shape=[shape(ROWS, FEAT), shape(ROWS, FEAT), shape(1, ROWS), shape(1, FEAT)],
        in_specs=[vmem] * 6,
        out_specs=[vmem] * 4,
    )(grad, by_row, by_col, weight, nr, nc)
    return nw, up, nr.reshape(ROWS), nc.reshape(FEAT)


def solution(mesh):
    return jax.shard_map(
        body,
        mesh=mesh,
        in_specs=(P("dp", "mp"), P("dp", "mp"), P("dp", "mp"), P("dp"), P("mp")),
        out_specs=(P("dp", "mp"), P("dp", "mp"), P("dp"), P("mp")),
        check_vma=False,
    )
```

```python
import jax
import jax.numpy as jnp
from jax import lax
from jax.experimental import pallas as pl
from jax.experimental.pallas import tpu as pltpu
from jax.sharding import PartitionSpec as P

D = 4096
STEPS_DONE = 10
MESH = pl.DeviceIdType.MESH

learn_rate = 0.01
tiny_eps = 1e-30
DECAY = 1.0 - STEPS_DONE ** (-0.8)

TOK = 768
FEAT = 1024
STEPS = 8
WIDE = 256
ROWS = 64


POWER = 16
TOP = 239.0


def coded(v):
    most = jnp.max(jnp.abs(v), axis=0, keepdims=True)
    scale = (most * 1.01 + 1e-30).astype(jnp.bfloat16)
    u = v * (TOP / scale.astype(jnp.float32))
    m = u * u
    m = m * m
    m = m * m
    m = m * m
    y = jnp.where(u < 0.0, -m, m).astype(jnp.bfloat16)
    return y, jnp.broadcast_to(scale, (16, v.shape[1]))


def decoded(y, scale):
    f = y.astype(jnp.float32)
    m = jnp.exp(jnp.log(jnp.abs(f)) * (1.0 / POWER))
    return jnp.where(f < 0.0, -m, m) * (scale.astype(jnp.float32)[:1] * (1.0 / TOP))


def kernel(
    a_ref, b_ref, rm_ref, cm_ref,
    grad_out, by_row_ref, by_col_ref, nr_ref, nc_ref,
    aa, bb, own, give, take, enc, in1, mid, in2, res, fin, grad,
    row_in, col_mine, col_in, col_mid, col_in2, sca_mine, sca_in, sca_mid, sca_in2,
    s_loc, s_a, r_a, s_b1, r_b1, s_b2, r_b2,
    s_core, r_core, s_1, r_1, s_2, r_2, s_z, r_z, s_row, s_col, r_row, r_col, s_col2, r_col2, s_sca, r_sca, s_sca2, r_sca2, heard,
):
    d = lax.axis_index("dp")
    c = lax.axis_index("mp")
    zh, x, y, core = d // 32, (d // 8) % 4, (d // 2) % 4, d % 2

    def dev(zh_, x_, y_, core_, c_):
        return (((zh_ * 4 + x_) * 4 + y_) * 2 + core_, c_)

    def plane_peer(j):
        q = lax.rem(x * 4 + y + j, 16)
        return dev(zh, q // 4, q % 4, core, c)

    def pole_peer(j):
        q = lax.rem((zh * 4 + c) * 2 + core + j, 16)
        return dev(q // 8, x, y, q % 2, (q // 2) % 4)

    def send(src, dst, s_sem, r_sem, to):
        return pltpu.make_async_remote_copy(
            src_ref=src, dst_ref=dst, send_sem=s_sem, recv_sem=r_sem, device_id=to, device_id_type=MESH
        )

    def arrived(ref, sem):
        pltpu.make_async_copy(ref, ref, sem).wait()

    up, down = lax.rem(zh * 4 + c + 1, 8), lax.rem(zh * 4 + c + 7, 8)
    neighbours = [
        dev(zh, x, y, 1 - core, c),
        dev(zh, lax.rem(x + 1, 4), y, core, c), dev(zh, lax.rem(x + 3, 4), y, core, c),
        dev(zh, x, lax.rem(y + 1, 4), core, c), dev(zh, x, lax.rem(y + 3, 4), core, c),
        dev(up // 4, x, y, core, up % 4), dev(down // 4, x, y, core, down % 4),
    ]
    barrier = pltpu.get_barrier_semaphore()
    for to in neighbours:
        pl.semaphore_signal(barrier, inc=1, device_id=to, device_id_type=MESH)
    pl.semaphore_wait(barrier, 7)

    def hail(k):
        for to in neighbours:
            pl.semaphore_signal(heard.at[k], inc=1, device_id=to, device_id_type=MESH)
        pl.semaphore_wait(heard.at[k], 7)

    edge = (c == 0) | (c == 3)
    half = lax.rem(c, 2)
    to_pair = dev(zh, x, y, core, c + 1 - 2 * half)
    to_mid = dev(zh, x, y, core, 3 - c)

    def a_copy(i):
        return send(a_ref.at[:, pl.ds(512 * i, 512)], aa.at[2 * half + i], s_a, r_a, to_pair)

    def b1_copy(i):
        return send(b_ref.at[:, pl.ds(WIDE * i, WIDE)], bb.at[i], s_b1, r_b1.at[i], to_mid)

    def piece(i):
        return pl.ds(192 * (i % 4), 192)

    def b_piece(i):
        return b_ref.at[piece(i), pl.ds(WIDE * (i // 4), WIDE)]

    def bb_piece(i):
        return bb.at[4 + i // 4, piece(i)]

    def b2_copy(i):
        return send(b_piece(i), bb_piece(i), s_b2, r_b2.at[i // 4], to_pair)

    def far_copy(i):
        return send(b_piece(i), bb_piece(i), s_b2, r_b2.at[i // 4], dev(zh, x, y, core, jnp.where(c == 0, 2, 1)))

    @pl.when(edge)
    def _():
        for i in range(2):
            a_copy(i).start()

    @pl.when(jnp.logical_not(edge))
    def _():
        for i in range(2):
            a_copy(i).start()
            b1_copy(2 * i).start()
            b1_copy(2 * i + 1).start()
        for i in range(16):
            b2_copy(i).start()

    def a_local(i):
        return pltpu.make_async_copy(a_ref.at[:, pl.ds(512 * i, 512)], aa.at[2 * half + i], s_loc.at[i])

    def b_local(i):
        return pltpu.make_async_copy(b_ref.at[:, pl.ds(WIDE * i, WIDE)], bb.at[i], s_loc.at[2 + i])

    for i in range(2):
        a_local(i).start()

    @pl.when(edge)
    def _():
        for i in range(4):
            b_local(i).start()

    hail(0)

    @pl.when(edge)
    def _():
        for i in range(16):
            far_copy(i).start()

    for k in range(1, 4):
        hail(k)

    @pl.when(edge)
    def _():
        for i in range(4):
            b_local(i).wait()

    for i in range(2):
        a_local(i).wait()
    arrived(aa.at[pl.ds(0, 2)], r_a)

    def core_copy(t):
        return send(give.at[t % 2], take.at[t], s_core.at[t % 2], r_core.at[t], dev(zh, x, y, 1 - core, c))

    def multiply(t):
        @pl.when((t < 4) & jnp.logical_not(edge))
        def _():
            for k in range(4):
                @pl.when(t == k)
                def _():
                    b1_copy(k).wait_recv()

        for k in range(4, 8):
            @pl.when(t == k)
            def _():
                arrived(bb.at[k], r_b2.at[k - 4])

        @pl.when(t >= 2)
        def _():
            core_copy(t - 2).wait_send()

        def of_x(xx, _):
            r = lax.dot_general(
                aa[xx], bb[t], (((0,), (0,)), ((), ())), preferred_element_type=jnp.float32
            )
            for yy in range(4):
                lo, hi = r[128 * yy : 128 * yy + 64], r[128 * yy + 64 : 128 * yy + 128]
                keep, go = jnp.where(core == 0, lo, hi), jnp.where(core == 0, hi, lo)
                own[t, 0, xx, yy] = keep[:, :128]
                own[t, 1, yy, xx] = keep[:, 128:]
                give[t % 2, 0, xx, yy] = go[:, :128]
                give[t % 2, 1, yy, xx] = go[:, 128:]
            return 0

        lax.fori_loop(0, 4, of_x, 0)
        core_copy(t).start()

    def copies_1(t):
        out = []
        for j in range(1, 4):
            out.append(send(enc.at[t, 0, lax.rem(x + j, 4)], in1.at[t, 0, j - 1], s_1.at[t], r_1.at[t],
                            dev(zh, lax.rem(x + j, 4), y, core, c)))
            out.append(send(enc.at[t, 1, lax.rem(y + j, 4)], in1.at[t, 1, j - 1], s_1.at[t], r_1.at[t],
                            dev(zh, x, lax.rem(y + j, 4), core, c)))
        return out

    def add_cores(t):
        core_copy(t).wait_recv()

        def of(k, _):
            h, q = k // 4, k % 4
            v = own[t, h, q] + take[t, h, q]
            mine = q == jnp.where(h == 0, x, y)

            @pl.when(mine)
            def _():
                own[t, h, q] = v

            @pl.when(jnp.logical_not(mine))
            def _():
                code, scale = coded(v.reshape(4 * ROWS, 128))
                enc[t, h, q, : 4 * ROWS] = code
                enc[t, h, q, 4 * ROWS :] = scale

            return 0

        lax.fori_loop(0, 8, of, 0)
        for q in copies_1(t):
            q.start()

    def copies_2(t):
        out = []
        for j in range(1, 4):
            out.append(send(mid.at[t, 0, lax.rem(y + j, 4)], in2.at[t, 0, j - 1], s_2.at[t], r_2.at[t], dev(zh, x, lax.rem(y + j, 4), core, c)))
            out.append(send(mid.at[t, 1, lax.rem(x + j, 4)], in2.at[t, 1, j - 1], s_2.at[t], r_2.at[t], dev(zh, lax.rem(x + j, 4), y, core, c)))
        return out

    def add_first(t):
        arrived(in1.at[t], r_1.at[t])

        def of(h, _):
            total = own[t, h, jnp.where(h == 0, x, y)].reshape(4 * ROWS, 128)
            for k in range(3):
                total = total + decoded(in1[t, h, k, : 4 * ROWS], in1[t, h, k, 4 * ROWS :])
            mid[t, h] = total.reshape(4, ROWS, 128)
            return 0

        lax.fori_loop(0, 2, of, 0)
        for q in copies_2(t):
            q.start()

    def target(t):
        return jnp.where(t < 4, jnp.where(edge, c, 3 - c), lax.rem(2 * c + 1, 5))

    def stays(t):
        return (zh == c // 2) & (target(t) == c)

    def z_copy(t):
        return send(res.at[t], fin.at[zh, lax.rem(t, 4)], s_z, r_z.at[zh],
                    dev(c // 2, x, y, core, target(t)))

    def add_second(t):
        arrived(in2.at[t], r_2.at[t])
        lo = mid[t, 0, y] + in2[t, 0, 0] + in2[t, 0, 1] + in2[t, 0, 2]
        hi = mid[t, 1, x] + in2[t, 1, 0] + in2[t, 1, 1] + in2[t, 1, 2]
        (lo, lo_scale), (hi, hi_scale) = coded(lo), coded(hi)

        def put(ref):
            ref[:ROWS, :128] = lo
            ref[:ROWS, 128:] = hi
            ref[ROWS:, :128] = lo_scale
            ref[ROWS:, 128:] = hi_scale

        @pl.when(stays(t))
        def _():
            put(fin.at[zh, lax.rem(t, 4)])

        @pl.when(jnp.logical_not(stays(t)))
        def _():
            put(res.at[t])
            z_copy(t).start()

    def when(cond, f, t):
        @pl.when(cond)
        def _():
            f(t)

    def step(s, _):
        when(s < 8, multiply, s)
        when((s >= 1) & (s < 9), add_cores, s - 1)
        when((s >= 3) & (s < 11), add_first, s - 3)
        when(s >= 5, add_second, s - 5)
        return 0

    lax.fori_loop(0, 13, step, 0)

    source = 2 * zh + c // 2
    for g in range(2):
        @pl.when(jnp.logical_not((zh == g) & (source == c)))
        def _():
            arrived(fin.at[g], r_z.at[g])
    row_sum = jnp.zeros((ROWS, 128), jnp.float32)
    for k in range(4):
        g = decoded(fin[0, k, :ROWS], fin[0, k, ROWS:]) + decoded(fin[1, k, :ROWS], fin[1, k, ROWS:])
        grad[:, pl.ds(WIDE * k, WIDE)] = g
        sq = g * g + tiny_eps
        row_sum = row_sum + sq[:, :128] + sq[:, 128:]
        col_mine[:, pl.ds(WIDE * k, WIDE)] = jnp.sum(sq, axis=0, keepdims=True)
    row_in[0] = row_sum
    grad_copy = pltpu.make_async_copy(grad, grad_out, s_loc.at[0])
    grad_copy.start()

    def row_copy(j):
        return send(row_in.at[0], row_in.at[j], s_row, r_row, dev(zh, x, y, core, lax.rem(c + j, 4)))

    def col_copy(j):
        return send(col_mine, col_in.at[j - 1], s_col, r_col, plane_peer(j))

    def col_copy2(j):
        q = lax.rem(zh * 2 + core + j, 4)
        return send(col_mid, col_in2.at[j - 1], s_col2, r_col2, dev(q // 2, x, y, q % 2, c))

    def each(lo, hi, f):
        def one(j, _):
            f(j)
            return 0
        lax.fori_loop(lo, hi, one, 0)

    each(1, 4, lambda j: row_copy(j).start())
    each(1, 16, lambda j: col_copy(j).start())
    eye = lax.broadcasted_iota(jnp.int32, (ROWS, ROWS), 0) == lax.broadcasted_iota(jnp.int32, (ROWS, ROWS), 1)
    rm = jnp.sum(jnp.where(eye, rm_ref[...], 0.0), axis=1, keepdims=True)
    arrived(row_in.at[pl.ds(1, 3)], r_row)
    rows = jnp.sum(row_in[0] + row_in[1] + row_in[2] + row_in[3], axis=1, keepdims=True)
    new_row = DECAY * rm + (1.0 - DECAY) * (rows / D)
    inverse = 1.0 / new_row
    for k in range(4):
        g = grad[:, pl.ds(WIDE * k, WIDE)]
        sca_mine[:, pl.ds(WIDE * k, WIDE)] = jnp.sum(g * g * inverse, axis=0, keepdims=True)
    sca_mine[:, FEAT:] = jnp.broadcast_to(jnp.sum(new_row, axis=0, keepdims=True), (1, 128))

    def sca_copy(j):
        return send(sca_mine, sca_in.at[j - 1], s_sca, r_sca, plane_peer(j))

    def sca_copy2(j):
        return send(sca_mid, sca_in2.at[j - 1], s_sca2, r_sca2, pole_peer(j))

    arrived(col_in, r_col)
    total = col_mine[...]
    for j in range(15):
        total = total + col_in[j]
    col_mid[...] = total
    each(1, 4, lambda j: col_copy2(j).start())
    each(1, 16, lambda j: sca_copy(j).start())
    nr_ref[...] = jnp.sum(jnp.where(eye, new_row, 0.0), axis=0, keepdims=True)
    root_r = 1.0 / jnp.sqrt(new_row)
    arrived(col_in2, r_col2)
    cols = col_mid[...] + col_in2[0] + col_in2[1] + col_in2[2]
    new_col = DECAY * cm_ref[...] + (1.0 - DECAY) * (cols / D)
    nc_ref[...] = new_col
    root_c = 1.0 / jnp.sqrt(new_col)
    by_col_ref[...] = root_c
    inverse = 1.0 / new_col
    arrived(sca_in, r_sca)
    total = sca_mine[...]
    for j in range(15):
        total = total + sca_in[j]
    part = jnp.sum(total[:, :FEAT] * inverse, axis=1, keepdims=True)
    lane = lax.broadcasted_iota(jnp.int32, (8, 128), 1)
    sca_mid[...] = jnp.where(lane == 0, part, jnp.where(lane == 1, total[:, FEAT:], 0.0))
    each(1, 16, lambda j: sca_copy2(j).start())
    arrived(sca_in2, r_sca2)
    total = sca_mid[...]
    for j in range(15):
        total = total + sca_in2[j]
    sum_sq = jnp.sum(jnp.where(lane == 0, total, 0.0), axis=1, keepdims=True)[:1]
    sum_row = jnp.sum(jnp.where(lane == 1, total, 0.0), axis=1, keepdims=True)[:1] / 4.0
    scale_total = sum_row / D
    root_mean = jnp.sqrt(sum_sq * scale_total / (D * D))
    factor = jnp.sqrt(scale_total) / jnp.maximum(1.0, root_mean)
    by_row_ref[...] = jnp.broadcast_to(root_r * factor, (ROWS, 128))

    grad_copy.wait()
    arrived(aa.at[pl.ds(0, 2)], s_a)
    arrived(bb.at[pl.ds(4, 4)], s_b2)

    @pl.when(jnp.logical_not(edge))
    def _():
        arrived(bb.at[pl.ds(0, 4)], s_b1)

    core_copy(6).wait_send()
    core_copy(7).wait_send()

    def sent(t):
        arrived(in1.at[t], s_1.at[t])
        arrived(in2.at[t], s_2.at[t])

        @pl.when(jnp.logical_not(stays(t)))
        def _():
            z_copy(t).wait_send()

    each(0, 8, sent)
    arrived(row_in.at[pl.ds(1, 3)], s_row)
    arrived(col_in, s_col)
    arrived(col_in2, s_col2)
    arrived(sca_in, s_sca)
    arrived(sca_in2, s_sca2)


def finish(grad_ref, by_row_ref, by_col_ref, w_ref, nr_in, nc_in, nw_ref, up_ref, nr_ref, nc_ref):
    scale = by_row_ref[...]
    for k in range(8):
        at = pl.ds(128 * k, 128)
        update = grad_ref[:, at] * scale * by_col_ref[:, at]
        up_ref[:, at] = update
        nw_ref[:, at] = w_ref[:, at] - learn_rate * update
    nr_ref[...] = nr_in[...]
    nc_ref[...] = nc_in[...]


def body(activations, out_grads, weight, row_moment, col_moment):
    f32, bf16 = jnp.float32, jnp.bfloat16
    V, S = pltpu.VMEM, pltpu.SemaphoreType.DMA
    vmem, hbm = pl.BlockSpec(memory_space=pltpu.VMEM), pl.BlockSpec(memory_space=pl.ANY)
    buffers = [
        V((4, TOK, 512), bf16),
        V((8, TOK, WIDE), bf16),
        V((STEPS, 2, 4, 4, ROWS, 128), f32),
        V((2, 2, 4, 4, ROWS, 128), f32),
        V((STEPS, 2, 4, 4, ROWS, 128), f32),
        V((STEPS, 2, 4, 4 * ROWS + 16, 128), bf16),
        V((STEPS, 2, 3, 4 * ROWS + 16, 128), bf16),
        V((STEPS, 2, 4, ROWS, 128), f32),
        V((STEPS, 2, 3, ROWS, 128), f32),
        V((STEPS, ROWS + 16, WIDE), bf16),
        V((2, 4, ROWS + 16, WIDE), bf16),
        V((ROWS, FEAT), f32),
        V((4, ROWS, 128), f32),
        V((1, FEAT), f32), V((15, 1, FEAT), f32), V((1, FEAT), f32), V((3, 1, FEAT), f32),
        V((1, FEAT + 128), f32), V((15, 1, FEAT + 128), f32), V((8, 128), f32), V((15, 8, 128), f32),
    ]
    sems = [S((6,)), S(()), S(()), S(()), S((4,)), S(()), S((4,)),
            S((2,)), S((8,)), S((8,)), S((8,)), S((8,)), S((8,)), S(()), S((2,))] + [S(())] * 10 + [pltpu.SemaphoreType.REGULAR((4,))]
    shape = lambda *dims: jax.ShapeDtypeStruct(dims, f32)
    grad, by_row, by_col, nr, nc = pl.pallas_call(
        kernel,
        out_shape=[shape(ROWS, FEAT), shape(ROWS, 128), shape(1, FEAT), shape(1, ROWS), shape(1, FEAT)],
        in_specs=[hbm, hbm, vmem, vmem],
        out_specs=[hbm, vmem, vmem, vmem, vmem],
        scratch_shapes=buffers + sems,
        compiler_params=pltpu.CompilerParams(
            collective_id=0, has_side_effects=True, vmem_limit_bytes=60 * 2**20
        ),
    )(activations, out_grads, row_moment.reshape(1, ROWS), col_moment.reshape(1, FEAT))
    nw, up, nr, nc = pl.pallas_call(
        finish,
        out_shape=[shape(ROWS, FEAT), shape(ROWS, FEAT), shape(1, ROWS), shape(1, FEAT)],
        in_specs=[vmem] * 6,
        out_specs=[vmem] * 4,
    )(grad, by_row, by_col, weight, nr, nc)
    return nw, up, nr.reshape(ROWS), nc.reshape(FEAT)


def solution(mesh):
    return jax.shard_map(
        body,
        mesh=mesh,
        in_specs=(P("dp", "mp"), P("dp", "mp"), P("dp", "mp"), P("dp"), P("mp")),
        out_specs=(P("dp", "mp"), P("dp", "mp"), P("dp"), P("mp")),
        check_vma=False,
    )
```

```python
import jax
import jax.numpy as jnp
from jax import lax
from jax.experimental import pallas as pl
from jax.experimental.pallas import tpu as pltpu
from jax.sharding import PartitionSpec as P

D = 4096
STEPS_DONE = 10
MESH = pl.DeviceIdType.MESH

learn_rate = 0.01
tiny_eps = 1e-30
DECAY = 1.0 - STEPS_DONE ** (-0.8)

TOK = 768
FEAT = 1024
CHUNKS = 8
WIDE = 256
NARROW = 128
LAG1, LAG2 = 3, 5
ROWS = 64
HALF = 32


POWER = 16
TOP = 239.0


def coded(v):
    most = jnp.max(jnp.abs(v), axis=0, keepdims=True)
    scale = (most * 1.01 + 1e-30).astype(jnp.bfloat16)
    u = v * (TOP / scale.astype(jnp.float32))
    m = u * u
    m = m * m
    m = m * m
    m = m * m
    y = jnp.where(u < 0.0, -m, m).astype(jnp.bfloat16)
    return y, jnp.broadcast_to(scale, (16, v.shape[1]))


def decoded(y, scale):
    f = y.astype(jnp.float32)
    m = jnp.exp(jnp.log(jnp.abs(f)) * (1.0 / POWER))
    return jnp.where(f < 0.0, -m, m) * (scale.astype(jnp.float32)[:1] * (1.0 / TOP))


def kernel(
    a_ref, b_ref, rm_ref, cm_ref,
    grad_out, by_row_ref, by_col_ref, nr_ref, nc_ref,
    aa, bb, bn, hown, hgive, htake, henc, hin1, hmid, hin2, own, give, take, enc, in1, mid, in2, whole, nres, res, fin, grad,
    row_in, col_mine, col_in, col_mid, col_in2, sca_mine, sca_in, sca_mid, sca_in2,
    s_loc, s_a, r_a, s_b1, r_b1, s_b2, r_b2,
    s_core, r_core, s_1, r_1, s_2, r_2, s_z, r_z, s_row, s_col, r_row, r_col, s_col2, r_col2, s_sca, r_sca, s_sca2, r_sca2, heard,
):
    d = lax.axis_index("dp")
    c = lax.axis_index("mp")
    zh, x, y, core = d // 32, (d // 8) % 4, (d // 2) % 4, d % 2

    def dev(zh_, x_, y_, core_, c_):
        return (((zh_ * 4 + x_) * 4 + y_) * 2 + core_, c_)

    def plane_peer(j):
        q = lax.rem(x * 4 + y + j, 16)
        return dev(zh, q // 4, q % 4, core, c)

    def pole_peer(j):
        q = lax.rem((zh * 4 + c) * 2 + core + j, 16)
        return dev(q // 8, x, y, q % 2, (q // 2) % 4)

    def send(src, dst, s_sem, r_sem, to):
        return pltpu.make_async_remote_copy(
            src_ref=src, dst_ref=dst, send_sem=s_sem, recv_sem=r_sem, device_id=to, device_id_type=MESH
        )

    def arrived(ref, sem):
        pltpu.make_async_copy(ref, ref, sem).wait()

    up, down = lax.rem(zh * 4 + c + 1, 8), lax.rem(zh * 4 + c + 7, 8)
    neighbours = [
        dev(zh, x, y, 1 - core, c),
        dev(zh, lax.rem(x + 1, 4), y, core, c), dev(zh, lax.rem(x + 3, 4), y, core, c),
        dev(zh, x, lax.rem(y + 1, 4), core, c), dev(zh, x, lax.rem(y + 3, 4), core, c),
        dev(up // 4, x, y, core, up % 4), dev(down // 4, x, y, core, down % 4),
    ]
    barrier = pltpu.get_barrier_semaphore()
    for to in neighbours:
        pl.semaphore_signal(barrier, inc=1, device_id=to, device_id_type=MESH)
    pl.semaphore_wait(barrier, 7)

    def hail(k):
        for to in neighbours:
            pl.semaphore_signal(heard.at[k], inc=1, device_id=to, device_id_type=MESH)
        pl.semaphore_wait(heard.at[k], 7)

    edge = (c == 0) | (c == 3)
    half = lax.rem(c, 2)
    to_pair = dev(zh, x, y, core, c + 1 - 2 * half)
    to_mid = dev(zh, x, y, core, 3 - c)

    def a_copy(i):
        return send(a_ref.at[:, pl.ds(512 * i, 512)], aa.at[2 * half + i], s_a, r_a, to_pair)

    def b1_copy(i):
        return send(b_ref.at[:, pl.ds(WIDE * i, WIDE)], bb.at[i], s_b1, r_b1.at[i], to_mid)

    def piece(i):
        return pl.ds(384 * (i % 2), 384)

    def b_piece(i):
        return b_ref.at[piece(i), pl.ds(NARROW * (i // 2), NARROW)]

    def bb_piece(i):
        return bn.at[i // 2, piece(i)]

    def b2_copy(i):
        return send(b_piece(i), bb_piece(i), s_b2, r_b2.at[i // 2], to_pair)

    def far_copy(i):
        return send(b_piece(i), bb_piece(i), s_b2, r_b2.at[i // 2], dev(zh, x, y, core, jnp.where(c == 0, 2, 1)))

    @pl.when(edge)
    def _():
        for i in range(2):
            a_copy(i).start()

    @pl.when(jnp.logical_not(edge))
    def _():
        for i in range(2):
            a_copy(i).start()
            b1_copy(2 * i).start()
            b1_copy(2 * i + 1).start()
        for i in range(16):
            b2_copy(i).start()

    def a_local(i):
        return pltpu.make_async_copy(a_ref.at[:, pl.ds(512 * i, 512)], aa.at[2 * half + i], s_loc.at[i])

    def b_local(i):
        return pltpu.make_async_copy(b_ref.at[:, pl.ds(WIDE * i, WIDE)], bb.at[i], s_loc.at[2 + i])

    for i in range(2):
        a_local(i).start()

    @pl.when(edge)
    def _():
        for i in range(4):
            b_local(i).start()

    hail(0)

    @pl.when(edge)
    def _():
        for i in range(16):
            far_copy(i).start()

    for k in range(1, 4):
        hail(k)

    @pl.when(edge)
    def _():
        for i in range(4):
            b_local(i).wait()

    for i in range(2):
        a_local(i).wait()

    sibling = dev(zh, x, y, 1 - core, c)

    def split(r, yy):
        lo, hi = r[128 * yy : 128 * yy + 64], r[128 * yy + 64 : 128 * yy + 128]
        return jnp.where(core == 0, lo, hi), jnp.where(core == 0, hi, lo)

    def product(xx, b):
        return lax.dot_general(aa[xx], b, (((0,), (0,)), ((), ())), preferred_element_type=jnp.float32)

    def half_core(u):
        return send(hgive.at[u % 2], htake.at[u], s_core.at[u % 2], r_core.at[u], sibling)

    def half_rows(u):
        return jnp.where(u < 4, half, 1 - half)

    def half_multiply(u):
        @pl.when(jnp.logical_not(edge))
        def _():
            for k in range(4):
                @pl.when(u == k)
                def _():
                    b1_copy(k).wait_recv()

        @pl.when(u == 4)
        def _():
            arrived(aa.at[pl.ds(0, 2)], r_a)

        @pl.when(u >= 2)
        def _():
            half_core(u - 2).wait_send()

        def of_x(k, _):
            r = product(2 * half_rows(u) + k, bb[u % 4])
            for yy in range(4):
                keep, go = split(r, yy)
                hown[u, yy, k] = keep
                hgive[u % 2, yy, k] = go
            return 0

        lax.fori_loop(0, 2, of_x, 0)
        half_core(u).start()

    def half_copies_1(u):
        return [
            send(henc.at[u, lax.rem(y + j, 4)], hin1.at[u, j - 1], s_1.at[u], r_1.at[u],
                 dev(zh, x, lax.rem(y + j, 4), core, c))
            for j in range(1, 4)
        ]

    def half_add_cores(u):
        half_core(u).wait_recv()

        def of(q, _):
            v = hown[u, q] + htake[u, q]

            @pl.when(q == y)
            def _():
                hown[u, q] = v

            @pl.when(q != y)
            def _():
                code, scale = coded(v.reshape(2 * ROWS, WIDE))
                henc[u, q, : 2 * ROWS] = code
                henc[u, q, 2 * ROWS :] = scale

            return 0

        lax.fori_loop(0, 4, of, 0)
        for q in half_copies_1(u):
            q.start()

    def half_copy_2(u, k):
        to = 2 * half_rows(u) + k
        j = lax.rem(to - x + 4, 4)
        return send(hmid.at[u, k], hin2.at[u % 4, j - 1], s_2.at[u % 4], r_2.at[u % 4], dev(zh, to, y, core, c))

    def half_add_first(u):
        arrived(hin1.at[u], r_1.at[u])
        total = hown[u, y].reshape(2 * ROWS, WIDE)
        for k in range(3):
            total = total + decoded(hin1[u, k, : 2 * ROWS], hin1[u, k, 2 * ROWS :])
        hmid[u] = total.reshape(2, ROWS, WIDE)
        for k in range(2):
            @pl.when(x != 2 * half_rows(u) + k)
            def _():
                half_copy_2(u, k).start()

    def half_add_second(u):
        @pl.when(x // 2 == half_rows(u))
        def _():
            t = u % 4
            arrived(hin2.at[t], r_2.at[t])
            total = hmid[u, x % 2] + hin2[t, 0] + hin2[t, 1] + hin2[t, 2]
            hand_over(t, total)

    def core_copy(t):
        return send(give.at[t % 2], take.at[t], s_core.at[t % 2], r_core.at[8 + t], sibling)

    def multiply(t):
        arrived(bn.at[t], r_b2.at[t])

        @pl.when(t < 2)
        def _():
            half_core(6 + t).wait_send()

        @pl.when(t >= 2)
        def _():
            core_copy(t - 2).wait_send()

        def of_x(xx, _):
            r = product(xx, bn[t])
            for yy in range(4):
                keep, go = split(r, yy)
                own[t, 0, xx, yy] = keep[:HALF]
                own[t, 1, yy, xx] = keep[HALF:]
                give[t % 2, 0, xx, yy] = go[:HALF]
                give[t % 2, 1, yy, xx] = go[HALF:]
            return 0

        lax.fori_loop(0, 4, of_x, 0)
        core_copy(t).start()

    def copies_1(t):
        out = []
        for j in range(1, 4):
            out.append(send(enc.at[t, 0, lax.rem(x + j, 4)], in1.at[t, 0, j - 1], s_1.at[8 + t], r_1.at[8 + t],
                            dev(zh, lax.rem(x + j, 4), y, core, c)))
            out.append(send(enc.at[t, 1, lax.rem(y + j, 4)], in1.at[t, 1, j - 1], s_1.at[8 + t], r_1.at[8 + t],
                            dev(zh, x, lax.rem(y + j, 4), core, c)))
        return out

    def add_cores(t):
        core_copy(t).wait_recv()

        def of(k, _):
            h, q = k // 4, k % 4
            v = own[t, h, q] + take[t, h, q]
            mine = q == jnp.where(h == 0, x, y)

            @pl.when(mine)
            def _():
                own[t, h, q] = v

            @pl.when(jnp.logical_not(mine))
            def _():
                code, scale = coded(v.reshape(4 * HALF, 128))
                enc[t, h, q, : 4 * HALF] = code
                enc[t, h, q, 4 * HALF :] = scale

            return 0

        lax.fori_loop(0, 8, of, 0)
        for q in copies_1(t):
            q.start()

    def copies_2(t):
        out = []
        for j in range(1, 4):
            out.append(send(mid.at[t, 0, lax.rem(y + j, 4)], in2.at[t, 0, j - 1], s_2.at[4 + t], r_2.at[4 + t], dev(zh, x, lax.rem(y + j, 4), core, c)))
            out.append(send(mid.at[t, 1, lax.rem(x + j, 4)], in2.at[t, 1, j - 1], s_2.at[4 + t], r_2.at[4 + t], dev(zh, lax.rem(x + j, 4), y, core, c)))
        return out

    def add_first(t):
        arrived(in1.at[t], r_1.at[8 + t])

        def of(h, _):
            total = own[t, h, jnp.where(h == 0, x, y)].reshape(4 * HALF, 128)
            for k in range(3):
                total = total + decoded(in1[t, h, k, : 4 * HALF], in1[t, h, k, 4 * HALF :])
            mid[t, h] = total.reshape(4, HALF, 128)
            return 0

        lax.fori_loop(0, 2, of, 0)
        for q in copies_2(t):
            q.start()

    def target(t):
        return jnp.where(t < 4, jnp.where(edge, c, 3 - c), lax.rem(2 * c + 1, 5))

    def stays(t):
        return (zh == c // 2) & (target(t) == c)

    def z_copy(t):
        return send(res.at[t], fin.at[zh, lax.rem(t, 4)], s_z, r_z.at[zh],
                    dev(c // 2, x, y, core, target(t)))

    def hand_over(t, total):
        code, scale = coded(total)

        @pl.when(stays(t))
        def _():
            fin[zh, t, :ROWS] = code
            fin[zh, t, ROWS:] = scale

        @pl.when(jnp.logical_not(stays(t)))
        def _():
            res[t, :ROWS] = code
            res[t, ROWS:] = scale
            z_copy(t).start()

    def narrow_copy(t):
        return send(nres.at[t], fin.at[zh, t // 2, :, pl.ds(pl.multiple_of(NARROW * (t % 2), NARROW), NARROW)], s_z, r_z.at[zh],
                    dev(c // 2, x, y, core, target(4)))

    def add_second(t):
        arrived(in2.at[t], r_2.at[4 + t])
        for h in range(2):
            at = pl.ds(HALF * h, HALF)
            whole[at] = mid[t, h, y if h == 0 else x] + in2[t, h, 0] + in2[t, h, 1] + in2[t, h, 2]
        code, scale = coded(whole[...])
        nres[t, :ROWS] = code
        nres[t, ROWS:] = scale
        narrow_copy(t).start()

    def when(cond, f, t):
        @pl.when(cond)
        def _():
            f(t)

    def step(s, _):
        when(s < 8, half_multiply, s)
        when((s >= 8) & (s < 16), multiply, s - 8)
        u = s - 1
        when((u >= 0) & (u < 8), half_add_cores, u)
        when((u >= 8) & (u < 16), add_cores, u - 8)
        u = s - LAG1
        when((u >= 0) & (u < 8), half_add_first, u)
        when((u >= 8) & (u < 16), add_first, u - 8)
        u = s - LAG2
        when((u >= 0) & (u < 8), half_add_second, u)
        when(u >= 8, add_second, u - 8)
        return 0

    lax.fori_loop(0, 16 + LAG2, step, 0)

    source = 2 * zh + c // 2
    for g in range(2):
        @pl.when(jnp.logical_not((zh == g) & (source == c)))
        def _():
            arrived(fin.at[g], r_z.at[g])
    row_sum = jnp.zeros((ROWS, 128), jnp.float32)
    for k in range(4):
        g = decoded(fin[0, k, :ROWS], fin[0, k, ROWS:]) + decoded(fin[1, k, :ROWS], fin[1, k, ROWS:])
        grad[:, pl.ds(WIDE * k, WIDE)] = g
        sq = g * g + tiny_eps
        row_sum = row_sum + sq[:, :128] + sq[:, 128:]
        col_mine[:, pl.ds(WIDE * k, WIDE)] = jnp.sum(sq, axis=0, keepdims=True)
    row_in[0] = row_sum
    grad_copy = pltpu.make_async_copy(grad, grad_out, s_loc.at[0])
    grad_copy.start()

    def row_copy(j):
        return send(row_in.at[0], row_in.at[j], s_row, r_row, dev(zh, x, y, core, lax.rem(c + j, 4)))

    def col_copy(j):
        return send(col_mine, col_in.at[j - 1], s_col, r_col, plane_peer(j))

    def col_copy2(j):
        q = lax.rem(zh * 2 + core + j, 4)
        return send(col_mid, col_in2.at[j - 1], s_col2, r_col2, dev(q // 2, x, y, q % 2, c))

    def each(lo, hi, f):
        def one(j, _):
            f(j)
            return 0
        lax.fori_loop(lo, hi, one, 0)

    each(1, 4, lambda j: row_copy(j).start())
    each(1, 16, lambda j: col_copy(j).start())
    eye = lax.broadcasted_iota(jnp.int32, (ROWS, ROWS), 0) == lax.broadcasted_iota(jnp.int32, (ROWS, ROWS), 1)
    rm = jnp.sum(jnp.where(eye, rm_ref[...], 0.0), axis=1, keepdims=True)
    arrived(row_in.at[pl.ds(1, 3)], r_row)
    rows = jnp.sum(row_in[0] + row_in[1] + row_in[2] + row_in[3], axis=1, keepdims=True)
    new_row = DECAY * rm + (1.0 - DECAY) * (rows / D)
    inverse = 1.0 / new_row
    for k in range(4):
        g = grad[:, pl.ds(WIDE * k, WIDE)]
        sca_mine[:, pl.ds(WIDE * k, WIDE)] = jnp.sum(g * g * inverse, axis=0, keepdims=True)
    sca_mine[:, FEAT:] = jnp.broadcast_to(jnp.sum(new_row, axis=0, keepdims=True), (1, 128))

    def sca_copy(j):
        return send(sca_mine, sca_in.at[j - 1], s_sca, r_sca, plane_peer(j))

    def sca_copy2(j):
        return send(sca_mid, sca_in2.at[j - 1], s_sca2, r_sca2, pole_peer(j))

    arrived(col_in, r_col)
    total = col_mine[...]
    for j in range(15):
        total = total + col_in[j]
    col_mid[...] = total
    each(1, 4, lambda j: col_copy2(j).start())
    each(1, 16, lambda j: sca_copy(j).start())
    nr_ref[...] = jnp.sum(jnp.where(eye, new_row, 0.0), axis=0, keepdims=True)
    root_r = 1.0 / jnp.sqrt(new_row)
    arrived(col_in2, r_col2)
    cols = col_mid[...] + col_in2[0] + col_in2[1] + col_in2[2]
    new_col = DECAY * cm_ref[...] + (1.0 - DECAY) * (cols / D)
    nc_ref[...] = new_col
    root_c = 1.0 / jnp.sqrt(new_col)
    by_col_ref[...] = root_c
    inverse = 1.0 / new_col
    arrived(sca_in, r_sca)
    total = sca_mine[...]
    for j in range(15):
        total = total + sca_in[j]
    part = jnp.sum(total[:, :FEAT] * inverse, axis=1, keepdims=True)
    lane = lax.broadcasted_iota(jnp.int32, (8, 128), 1)
    sca_mid[...] = jnp.where(lane == 0, part, jnp.where(lane == 1, total[:, FEAT:], 0.0))
    each(1, 16, lambda j: sca_copy2(j).start())
    arrived(sca_in2, r_sca2)
    total = sca_mid[...]
    for j in range(15):
        total = total + sca_in2[j]
    sum_sq = jnp.sum(jnp.where(lane == 0, total, 0.0), axis=1, keepdims=True)[:1]
    sum_row = jnp.sum(jnp.where(lane == 1, total, 0.0), axis=1, keepdims=True)[:1] / 4.0
    scale_total = sum_row / D
    root_mean = jnp.sqrt(sum_sq * scale_total / (D * D))
    factor = jnp.sqrt(scale_total) / jnp.maximum(1.0, root_mean)
    by_row_ref[...] = jnp.broadcast_to(root_r * factor, (ROWS, 128))

    grad_copy.wait()
    arrived(aa.at[pl.ds(0, 2)], s_a)
    arrived(bn, s_b2)

    @pl.when(jnp.logical_not(edge))
    def _():
        arrived(bb, s_b1)

    core_copy(6).wait_send()
    core_copy(7).wait_send()

    def sent(t):
        arrived(hin1.at[t], s_1.at[t])
        arrived(in1.at[t], s_1.at[8 + t])
        arrived(in2.at[t], s_2.at[4 + t])
        narrow_copy(t).wait_send()

        @pl.when(t < 4)
        def _():
            arrived(hin2.at[t], s_2.at[t])

            @pl.when(jnp.logical_not(stays(t)))
            def _():
                z_copy(t).wait_send()

    each(0, 8, sent)
    arrived(row_in.at[pl.ds(1, 3)], s_row)
    arrived(col_in, s_col)
    arrived(col_in2, s_col2)
    arrived(sca_in, s_sca)
    arrived(sca_in2, s_sca2)


def finish(grad_ref, by_row_ref, by_col_ref, w_ref, nr_in, nc_in, nw_ref, up_ref, nr_ref, nc_ref):
    scale = by_row_ref[...]
    for k in range(8):
        at = pl.ds(128 * k, 128)
        update = grad_ref[:, at] * scale * by_col_ref[:, at]
        up_ref[:, at] = update
        nw_ref[:, at] = w_ref[:, at] - learn_rate * update
    nr_ref[...] = nr_in[...]
    nc_ref[...] = nc_in[...]


def body(activations, out_grads, weight, row_moment, col_moment):
    f32, bf16 = jnp.float32, jnp.bfloat16
    V, S = pltpu.VMEM, pltpu.SemaphoreType.DMA
    vmem, hbm = pl.BlockSpec(memory_space=pltpu.VMEM), pl.BlockSpec(memory_space=pl.ANY)
    buffers = [
        V((4, TOK, 512), bf16),
        V((4, TOK, WIDE), bf16),
        V((CHUNKS, TOK, NARROW), bf16),
        V((8, 4, 2, ROWS, WIDE), f32),
        V((2, 4, 2, ROWS, WIDE), f32),
        V((8, 4, 2, ROWS, WIDE), f32),
        V((8, 4, 2 * ROWS + 16, WIDE), bf16),
        V((8, 3, 2 * ROWS + 16, WIDE), bf16),
        V((8, 2, ROWS, WIDE), f32),
        V((4, 3, ROWS, WIDE), f32),
        V((CHUNKS, 2, 4, 4, HALF, 128), f32),
        V((2, 2, 4, 4, HALF, 128), f32),
        V((CHUNKS, 2, 4, 4, HALF, 128), f32),
        V((CHUNKS, 2, 4, 4 * HALF + 16, 128), bf16),
        V((CHUNKS, 2, 3, 4 * HALF + 16, 128), bf16),
        V((CHUNKS, 2, 4, HALF, 128), f32),
        V((CHUNKS, 2, 3, HALF, 128), f32),
        V((ROWS, NARROW), f32),
        V((CHUNKS, ROWS + 16, NARROW), bf16),
        V((4, ROWS + 16, WIDE), bf16),
        V((2, 4, ROWS + 16, WIDE), bf16),
        V((ROWS, FEAT), f32),
        V((4, ROWS, 128), f32),
        V((1, FEAT), f32), V((15, 1, FEAT), f32), V((1, FEAT), f32), V((3, 1, FEAT), f32),
        V((1, FEAT + 128), f32), V((15, 1, FEAT + 128), f32), V((8, 128), f32), V((15, 8, 128), f32),
    ]
    sems = [S((6,)), S(()), S(()), S(()), S((4,)), S(()), S((8,)),
            S((2,)), S((16,)), S((16,)), S((16,)), S((12,)), S((12,)), S(()), S((2,))] + [S(())] * 10 + [pltpu.SemaphoreType.REGULAR((4,))]
    shape = lambda *dims: jax.ShapeDtypeStruct(dims, f32)
    grad, by_row, by_col, nr, nc = pl.pallas_call(
        kernel,
        out_shape=[shape(ROWS, FEAT), shape(ROWS, 128), shape(1, FEAT), shape(1, ROWS), shape(1, FEAT)],
        in_specs=[hbm, hbm, vmem, vmem],
        out_specs=[hbm, vmem, vmem, vmem, vmem],
        scratch_shapes=buffers + sems,
        compiler_params=pltpu.CompilerParams(
            collective_id=0, has_side_effects=True, vmem_limit_bytes=60 * 2**20
        ),
    )(activations, out_grads, row_moment.reshape(1, ROWS), col_moment.reshape(1, FEAT))
    nw, up, nr, nc = pl.pallas_call(
        finish,
        out_shape=[shape(ROWS, FEAT), shape(ROWS, FEAT), shape(1, ROWS), shape(1, FEAT)],
        in_specs=[vmem] * 6,
        out_specs=[vmem] * 4,
    )(grad, by_row, by_col, weight, nr, nc)
    return nw, up, nr.reshape(ROWS), nc.reshape(FEAT)


def solution(mesh):
    return jax.shard_map(
        body,
        mesh=mesh,
        in_specs=(P("dp", "mp"), P("dp", "mp"), P("dp", "mp"), P("dp"), P("mp")),
        out_specs=(P("dp", "mp"), P("dp", "mp"), P("dp"), P("mp")),
        check_vma=False,
    )
```
